256 devices in a mesh: tm: 8 (over y, z_lo), space: 32 (over z_hi, x, core).
Axes of the slice: x: 4, y: 4, z: 8 (z_hi: 4, z_lo: 2; z = z_hi * 2 + z_lo), core: 2. Of those that a mesh axis runs over, the one named last changes fastest.
Arguments:
- queries: bfloat16 [8, 4096, 512], P('tm', 'space'), may hold values from -120 to 120
- keys: bfloat16 [8, 4096, 512], P('tm', 'space'), may hold values from -8 to 8
- values: bfloat16 [8, 4096, 512], P('tm', 'space'), may hold values from -6 to 6
- w_query: bfloat16 [512, 512], replicated, may hold values from -0.25 to 0.25
- w_key: bfloat16 [512, 512], replicated, may hold values from -0.25 to 0.25
- w_value: bfloat16 [512, 512], replicated, may hold values from -0.25 to 0.25
- grad_out: bfloat16 [8, 4096, 512], P('tm', 'space'), may hold values from -6 to 6
- tile_list: int32 [8, 32, 8, 2], replicated, may hold values from 0 to 63, as said below
- tile_count: int32 [8, 32, 8], replicated, may hold values from 1 to 2
Outputs:
- mixed: bfloat16 [8, 4096, 512], P('tm', 'space')
- grad_queries: bfloat16 [8, 4096, 512], P('tm', 'space')
- grad_keys: bfloat16 [8, 4096, 512], P('tm', 'space')
- grad_values: bfloat16 [8, 4096, 512], P('tm', 'space')
The draws below stay inside these ranges and needn't reach their ends.
Inputs may be any that keep to these rules, and one draw needn't show every extreme that they name: For one query frame t and the query blocks of one index s of space (blocks s * 1 to (s + 1) * 1 - 1), the entries of tile_list for all key frames and slots, live or not, name tiles whose owner, tile // 2, occurs at most once; in every query frame one owner (the same for all indices s) is named exactly once by the lists of every index s.
All inputs are finite; a program needn't handle non-finite values.
Results may differ from the reference program's by a relative error of at most 0.015.
Values may be sent and summed in bfloat16 or wider, within the bound.
No kernel may reach another device: no remote copies, remote signals or barrier semaphores. Data moves between devices by JAX's collectives and lax.ppermute only.
A program may use at most 64 MiB of HBM per device.

```python
import jax
import jax.numpy as jnp
from jax import lax

D = 512
HEAD = 64
HEADS = 8
TILE = 64
BLOCK = 2
SLOTS = 2
TILE_DEV = 2
FRAMES = 8
TILES = 64
BLOCKS = 32
POSITIONS = 4096
MOST = 1


def shared_base(key):
    return jax.random.normal(jax.random.fold_in(key, 99), (TILES * TILE, D), jnp.float32)


def draw_queries(key, part):
    common = shared_base(key)
    key = jax.random.fold_in(key, 1)
    noise = jax.random.normal(key, (FRAMES, TILES * TILE, D), jnp.float32)
    result = 0.8 * common[None] + 0.6 * noise
    return jnp.clip(result, -120.0, 120.0).astype(jnp.bfloat16)


def draw_keys(key, part):
    common = shared_base(key)
    key = jax.random.fold_in(key, 2)
    noise = jax.random.normal(key, (FRAMES, TILES * TILE, D), jnp.float32)
    result = 0.8 * common[None] + 0.6 * noise
    return jnp.clip(result, -8.0, 8.0).astype(jnp.bfloat16)


def shuffle_row(row_key, count):
    return jax.random.permutation(row_key, count)


def partial_perm(count):

    def permute(row_key):
        return shuffle_row(row_key, count)
    return permute


def draw_tile_list(key, part):
    key = jax.random.fold_in(key, 7)
    space_count = TILES // TILE_DEV
    block_dev = TILE_DEV // BLOCK
    positions = block_dev * FRAMES * SLOTS
    groups = FRAMES * space_count
    first_keys = jax.random.split(jax.random.fold_in(key, 1), groups)
    second_keys = jax.random.split(jax.random.fold_in(key, 2), groups)
    orders = jax.vmap(partial_perm(space_count))(first_keys)
    hottest = jax.random.randint(jax.random.fold_in(key, 4), (FRAMES, 1), 0, space_count)
    hottest = jnp.repeat(hottest, space_count, axis=0)
    leading = orders[:, :1]
    orders = jnp.where(orders == hottest, leading, orders)
    front = jnp.arange(space_count, dtype=jnp.int32)[None, :] == 0
    orders = jnp.where(front, hottest, orders)
    spread = jnp.arange(positions, dtype=jnp.int32) // MOST % space_count
    owners = orders[:, spread]
    shuffles = jax.vmap(partial_perm(positions))(second_keys)
    owners = jnp.take_along_axis(owners, shuffles, axis=1)
    within = jax.random.randint(jax.random.fold_in(key, 3), (groups, positions), 0, TILE_DEV)
    chosen = owners * TILE_DEV + within
    return chosen.reshape(FRAMES, TILES // BLOCK, FRAMES, SLOTS).astype(jnp.int32)


def touch_ends(entries, own_key, low, high):
    longest = entries.shape.index(max(entries.shape))
    spots = []
    for shift in (0, 1):
        where = [jax.random.randint(jax.random.fold_in(own_key, axis), (), 0, length) for axis, length in enumerate(entries.shape)]
        where[longest] = (where[longest] + shift) % entries.shape[longest]
        spots.append(tuple(where))
    return entries.at[spots[0]].set(low).at[spots[1]].set(high)


def block_scale(own_key, extent, cuts, smallest, top_value):
    loudness = 1.0
    for axis_at, blocks in cuts:
        heights = jax.random.uniform(jax.random.fold_in(jax.random.fold_in(own_key, 6), axis_at), (blocks,), jnp.float32, smallest / len(cuts), top_value / len(cuts))
        loudness = loudness * jnp.repeat(jnp.exp(heights), extent[axis_at] // blocks).reshape((-1,) + (1,) * (len(extent) - 1 - axis_at))
    return loudness


def centred(stream_key, extent, width, most, pieces=(), kind=jnp.bfloat16):
    values = jax.random.normal(stream_key, extent, jnp.float32) * width
    if len(pieces) > 0:
        values = block_scale(stream_key, extent, pieces, -0.22, 0.18) * values
    return jnp.clip(values, min=-most, max=most).astype(kind)


def setup_inputs(seed: int = 0) -> dict:
    splits = jax.random.split(jax.random.key(seed), 10)
    queries = draw_queries(jax.random.fold_in(splits[9], 71), 0)
    keys = draw_keys(jax.random.fold_in(splits[9], 71), 0)
    values = centred(splits[2], (FRAMES, POSITIONS, D), 1.0, 6.0, ((0, 8), (1, 32)))
    w_query = centred(splits[3], (D, D), D ** -0.5, 0.25)
    w_key = centred(splits[4], (D, D), D ** -0.5, 0.25)
    w_value = centred(splits[5], (D, D), D ** -0.5, 0.25)
    grad_out = centred(splits[6], (FRAMES, POSITIONS, D), 1.0, 6.0, ((0, 8), (1, 32)))
    tile_list = draw_tile_list(jax.random.fold_in(splits[9], 71), 0)
    tile_count = touch_ends(jax.random.randint(splits[8], (FRAMES, BLOCKS, FRAMES), 1, SLOTS + 1), jax.random.fold_in(splits[8], 1), 1, SLOTS).astype(jnp.int32)
    return {"queries": queries, "keys": keys, "values": values, "w_query": w_query, "w_key": w_key, "w_value": w_value, "grad_out": grad_out, "tile_list": tile_list, "tile_count": tile_count}


score_scale = 0.125


def pool_frames(traj_rows, frame_now, w_query, w_key, w_value, grad_rows):
    query_count, frame_count, model_width = traj_rows.shape
    highest = lax.Precision.HIGHEST
    own_rows = lax.dynamic_index_in_dim(traj_rows, frame_now, 1, keepdims=False)
    pooled_q = jnp.dot(own_rows, w_query, preferred_element_type=jnp.float32).reshape(query_count, HEADS, HEAD)
    flat_rows = traj_rows.reshape(query_count * frame_count, model_width)
    pooled_k = jnp.dot(flat_rows, w_key, preferred_element_type=jnp.float32).reshape(query_count, frame_count, HEADS, HEAD)
    pooled_v = jnp.dot(flat_rows, w_value, preferred_element_type=jnp.float32).reshape(query_count, frame_count, HEADS, HEAD)
    logits = jnp.einsum("qhe,qfhe->qhf", pooled_q, pooled_k, precision=highest) * score_scale
    raised = jnp.exp(logits)
    frame_weights = raised / jnp.sum(raised, axis=-1, keepdims=True)
    mixed_rows = jnp.einsum("qhf,qfhe->qhe", frame_weights, pooled_v, precision=highest)
    mixed_rows = mixed_rows.reshape(query_count, model_width).astype(jnp.bfloat16)
    upstream = grad_rows.astype(jnp.float32).reshape(query_count, HEADS, HEAD)
    grad_pv = jnp.einsum("qhf,qhe->qfhe", frame_weights, upstream, precision=highest)
    grad_fw = jnp.einsum("qhe,qfhe->qhf", upstream, pooled_v, precision=highest)
    inner = jnp.sum(frame_weights * grad_fw, axis=-1, keepdims=True)
    grad_logit = frame_weights * (grad_fw - inner) * score_scale
    grad_pq = jnp.einsum("qhf,qfhe->qhe", grad_logit, pooled_k, precision=highest).astype(jnp.bfloat16)
    grad_pk = jnp.einsum("qhf,qhe->qfhe", grad_logit, pooled_q, precision=highest).astype(jnp.bfloat16)
    grad_pv = grad_pv.astype(jnp.bfloat16)
    grad_traj = jnp.dot(grad_pk.reshape(query_count * frame_count, model_width), w_key.T, preferred_element_type=jnp.float32)
    grad_traj = grad_traj + jnp.dot(grad_pv.reshape(query_count * frame_count, model_width), w_value.T, preferred_element_type=jnp.float32)
    grad_traj = grad_traj.reshape(query_count, frame_count, model_width)
    own_term = jnp.dot(grad_pq.reshape(query_count, model_width), w_query.T, preferred_element_type=jnp.float32)
    picker = (jnp.arange(frame_count, dtype=jnp.int32) == frame_now).astype(jnp.float32)
    grad_traj = grad_traj + picker[None, :, None] * own_term[:, None, :]
    return mixed_rows, grad_traj.astype(jnp.bfloat16)


def reference(queries, keys, values, w_query, w_key, w_value, grad_out, tile_list, tile_count):
    key_tiles = keys.reshape(FRAMES, TILES, TILE, D)
    value_tiles = values.reshape(FRAMES, TILES, TILE, D)
    frame_column = jnp.arange(FRAMES, dtype=jnp.int32)[:, None]
    frame_ids = jnp.arange(FRAMES, dtype=jnp.int32)[None, :, None]
    slot_numbers = jnp.arange(SLOTS, dtype=jnp.int32)
    block_len = BLOCK * TILE

    def block_slots(block_list):
        key_slots = key_tiles[frame_column, block_list].reshape(FRAMES, SLOTS * TILE, HEADS, HEAD).astype(jnp.float32)
        value_slots = value_tiles[frame_column, block_list].reshape(FRAMES, SLOTS * TILE, HEADS, HEAD).astype(jnp.float32)
        return key_slots, value_slots

    def block_softmax(query_block, key_slots, block_count):
        live_mask = jnp.repeat(slot_numbers[None, :] < block_count[:, None], TILE, axis=1)
        scores = jnp.einsum("qhe,fkhe->qfhk", query_block, key_slots) * score_scale
        scores = jnp.where(live_mask[None, :, None, :], scores, -jnp.inf)
        raised = jnp.exp(scores - jnp.max(scores, axis=-1, keepdims=True))
        weights_f = raised / jnp.sum(raised, axis=-1, keepdims=True)
        weights_b = lax.optimization_barrier(weights_f.astype(jnp.bfloat16)).astype(jnp.float32)
        return weights_f, weights_b

    def one_frame(carry, frame_now):
        sum_keys, sum_values = carry
        lists = tile_list[frame_now]
        counts = tile_count[frame_now]
        query_blocks = queries[frame_now].reshape(BLOCKS, block_len, HEADS, HEAD).astype(jnp.float32)

        def forward_block(inputs):
            query_block, block_list, block_count = inputs
            key_slots, value_slots = block_slots(block_list)
            weights_f, weights_b = block_softmax(query_block, key_slots, block_count)
            return jnp.einsum("qfhk,fkhe->qfhe", weights_b, value_slots).astype(jnp.bfloat16)

        trajectory = lax.map(forward_block, (query_blocks, lists, counts))
        traj_rows = trajectory.reshape(POSITIONS, FRAMES, D)
        mixed_rows, grad_traj = pool_frames(traj_rows, frame_now, w_query, w_key, w_value, grad_out[frame_now])
        grad_blocks = grad_traj.reshape(BLOCKS, block_len, FRAMES, HEADS, HEAD).astype(jnp.float32)

        def backward_block(inputs):
            query_block, block_list, block_count, grad_block = inputs
            key_slots, value_slots = block_slots(block_list)
            weights_f, weights_b = block_softmax(query_block, key_slots, block_count)
            grad_w = jnp.einsum("qfhe,fkhe->qfhk", grad_block, value_slots)
            inner = jnp.sum(weights_f * grad_w, axis=-1, keepdims=True)
            grad_s = lax.optimization_barrier((weights_f * (grad_w - inner) * score_scale).astype(jnp.bfloat16)).astype(jnp.float32)
            grad_q = jnp.einsum("qfhk,fkhe->qhe", grad_s, key_slots).astype(jnp.bfloat16)
            slot_dk = jnp.einsum("qfhk,qhe->fkhe", grad_s, query_block).astype(jnp.bfloat16)
            slot_dv = jnp.einsum("qfhk,qfhe->fkhe", weights_b, grad_block).astype(jnp.bfloat16)
            return grad_q, slot_dk, slot_dv

        grad_q, slot_dk, slot_dv = lax.map(backward_block, (query_blocks, lists, counts, grad_blocks))
        segments = (frame_ids * TILES + lists).reshape(-1)
        frame_dk = jax.ops.segment_sum(slot_dk.reshape(BLOCKS * FRAMES * SLOTS, TILE * D).astype(jnp.float32), segments, FRAMES * TILES)
        frame_dv = jax.ops.segment_sum(slot_dv.reshape(BLOCKS * FRAMES * SLOTS, TILE * D).astype(jnp.float32), segments, FRAMES * TILES)
        frame_dk = lax.optimization_barrier(frame_dk.astype(jnp.bfloat16))
        frame_dv = lax.optimization_barrier(frame_dv.astype(jnp.bfloat16))
        carry = (sum_keys + frame_dk.astype(jnp.float32), sum_values + frame_dv.astype(jnp.float32))
        return carry, (mixed_rows, grad_q.reshape(POSITIONS, D))

    start = jnp.zeros((FRAMES * TILES, TILE * D), jnp.float32)
    (sum_keys, sum_values), (mixed, grad_queries) = lax.scan(one_frame, (start, start), jnp.arange(FRAMES, dtype=jnp.int32))
    grad_keys = sum_keys.reshape(FRAMES, POSITIONS, D).astype(jnp.bfloat16)
    grad_values = sum_values.reshape(FRAMES, POSITIONS, D).astype(jnp.bfloat16)
    return (mixed, grad_queries, grad_keys, grad_values)
```

```python
import functools

import jax
import jax.numpy as jnp
from jax import lax
from jax.experimental import pallas as pl
from jax.experimental.pallas import tpu as pltpu
from jax.sharding import Mesh
from jax.sharding import PartitionSpec as P

HEAD = 64
HEADS = 8
TILE = 64
FRAMES = 8
SLOTS = 2
WIDTH = 512
PAIRS = 4
ROWS = 128
SCALE = 0.125
TM = ("y", "zl")
SPACE = ("zh", "x", "c")
VMEM_LIMIT = 50 * 1024 * 1024


def params():
    return pltpu.CompilerParams(vmem_limit_bytes=VMEM_LIMIT)


def vmem():
    return pl.BlockSpec(memory_space=pltpu.VMEM)


def smem():
    return pl.BlockSpec(memory_space=pltpu.SMEM)


def hbm():
    return pl.BlockSpec(memory_space=pl.ANY)


def shift(value, axis, step):
    size = lax.axis_size(axis)
    return lax.ppermute(value, axis, [(i, (i + step) % size) for i in range(size)])


def gather_frame(own):
    from_down = shift(own, "zh", 1)
    from_up = shift(own, "zh", -1)
    far_low = shift(from_down[0:1], "zh", 1)
    far_high = shift(from_up[1:2], "zh", -1)
    column = jnp.concatenate([own, from_up, far_low, far_high, from_down], axis=0)
    from_left = shift(column, "x", 1)
    from_right = shift(column, "x", -1)
    across_low = shift(from_left[0:4], "x", 1)
    across_high = shift(from_right[4:8], "x", -1)
    mine = [column, from_right, across_low, across_high, from_left]
    theirs = [shift(piece, "c", 1) for piece in mine]
    return mine + theirs


def select_kernel(piece_ref, row_ref, *refs):
    pieces, out_ref, sems = refs[:10], refs[10], refs[11]

    @pl.loop(0, FRAMES * SLOTS)
    def _(slot):
        which = piece_ref[slot]
        row = row_ref[slot]
        for number, piece in enumerate(pieces):

            @pl.when(which == number)
            def _():
                pltpu.make_async_copy(
                    piece.at[pl.ds(row, 1)], out_ref.at[pl.ds(slot, 1)], sems.at[slot]
                ).start()

    @pl.loop(0, FRAMES * SLOTS)
    def _(slot):
        pltpu.make_async_copy(
            pieces[0].at[pl.ds(0, 1)], out_ref.at[pl.ds(slot, 1)], sems.at[slot]
        ).wait()


def select_tiles(piece_ids, piece_rows, pieces):
    return pl.pallas_call(
        select_kernel,
        out_shape=jax.ShapeDtypeStruct((FRAMES * SLOTS, TILE, WIDTH), jnp.bfloat16),
        in_specs=[smem(), smem()] + [hbm()] * 10,
        out_specs=hbm(),
        scratch_shapes=[pltpu.SemaphoreType.DMA((FRAMES * SLOTS,))],
        compiler_params=params(),
        name="select_tiles",
    )(piece_ids, piece_rows, *pieces)


def split_heads(pair):
    rows = lax.broadcasted_iota(jnp.int32, pair.shape, 0)
    zero = jnp.zeros_like(pair)
    return jnp.concatenate(
        [jnp.where(rows < HEAD, pair, zero), jnp.where(rows >= HEAD, pair, zero)], axis=1
    )


def join_heads(both):
    return jnp.concatenate([both[:HEAD, :ROWS], both[HEAD:, ROWS:]], axis=0)


def dot_nn(a, b):
    return jnp.dot(a, b, preferred_element_type=jnp.float32)


def dot_tn(a, b):
    return lax.dot_general(a, b, (((0,), (0,)), ((), ())), preferred_element_type=jnp.float32)


def dot_nt(a, b):
    return lax.dot_general(a, b, (((1,), (1,)), ((), ())), preferred_element_type=jnp.float32)


def weights_kernel(count_ref, query_ref, key_ref, weight_ref):
    frame = pl.program_id(0)
    limit = count_ref[frame] * TILE
    rows = lax.broadcasted_iota(jnp.int32, (ROWS, 2 * ROWS), 0)
    live = rows < limit
    for pair in range(PAIRS):
        lanes = slice(pair * 128, pair * 128 + 128)
        scores = dot_nn(key_ref[0, :, lanes], split_heads(query_ref[lanes, :])) * SCALE
        scores = jnp.where(live, scores, -jnp.inf)
        raised = jnp.exp(scores - jnp.max(scores, axis=0, keepdims=True))
        weight_ref[0, pair] = raised / jnp.sum(raised, axis=0, keepdims=True)


def attend_weights(counts, query_t, keys):
    return pl.pallas_call(
        weights_kernel,
        grid=(FRAMES,),
        out_shape=jax.ShapeDtypeStruct((FRAMES, PAIRS, ROWS, 2 * ROWS), jnp.float32),
        in_specs=[
            smem(),
            pl.BlockSpec((WIDTH, ROWS), lambda f: (0, 0)),
            pl.BlockSpec((1, ROWS, WIDTH), lambda f: (f, 0, 0)),
        ],
        out_specs=pl.BlockSpec((1, PAIRS, ROWS, 2 * ROWS), lambda f: (f, 0, 0, 0)),
        compiler_params=params(),
        name="attend_weights",
    )(counts, query_t, keys)


def pool_kernel(
    frame_ref,
    weight_ref,
    value_ref,
    wq_ref,
    wk_ref,
    wv_ref,
    wqt_ref,
    wkt_ref,
    wvt_ref,
    go_ref,
    mixed_ref,
    gt_ref,
    dv_ref,
    traj,
    pooled_k,
    pooled_v,
    pooled_q,
    grad_pk,
    grad_pv,
    grad_pq,
    total,
):
    for frame in range(FRAMES):
        for pair in range(PAIRS):
            lanes = slice(pair * 128, pair * 128 + 128)
            both = dot_tn(value_ref[frame, :, lanes], weight_ref[frame, pair].astype(jnp.bfloat16))
            traj[lanes, frame * ROWS : (frame + 1) * ROWS] = join_heads(both).astype(jnp.bfloat16)
    own = pl.ds(pl.multiple_of(frame_ref[0] * ROWS, ROWS), ROWS)
    pooled_q[...] = dot_nn(wqt_ref[...], traj[:, own])
    pooled_k[...] = dot_nn(wkt_ref[...], traj[...])
    pooled_v[...] = dot_nn(wvt_ref[...], traj[...])
    for head in range(HEADS):
        rows = slice(head * HEAD, (head + 1) * HEAD)
        query = pooled_q[rows, :]
        upstream = go_ref[rows, :].astype(jnp.float32)
        columns = [slice(f * ROWS, (f + 1) * ROWS) for f in range(FRAMES)]
        logits = jnp.concatenate(
            [
                jnp.sum(query * pooled_k[rows, columns[f]], axis=0, keepdims=True)
                for f in range(FRAMES)
            ],
            axis=0,
        )
        raised = jnp.exp(logits * SCALE)
        fw = raised / jnp.sum(raised, axis=0, keepdims=True)
        grad_fw = jnp.concatenate(
            [
                jnp.sum(upstream * pooled_v[rows, columns[f]], axis=0, keepdims=True)
                for f in range(FRAMES)
            ],
            axis=0,
        )
        inner = jnp.sum(fw * grad_fw, axis=0, keepdims=True)
        grad_logit = fw * (grad_fw - inner) * SCALE
        mixed = jnp.zeros((HEAD, ROWS), jnp.float32)
        grad_query = jnp.zeros((HEAD, ROWS), jnp.float32)
        for f in range(FRAMES):
            weight = fw[f : f + 1, :]
            slope = grad_logit[f : f + 1, :]
            mixed = mixed + weight * pooled_v[rows, columns[f]]
            grad_query = grad_query + slope * pooled_k[rows, columns[f]]
            grad_pk[rows, columns[f]] = (slope * query).astype(jnp.bfloat16)
            grad_pv[rows, columns[f]] = (weight * upstream).astype(jnp.bfloat16)
        mixed_ref[rows, :] = mixed.astype(jnp.bfloat16)
        grad_pq[rows, :] = grad_query.astype(jnp.bfloat16)
    total[...] = dot_nn(wk_ref[...], grad_pk[...]) + dot_nn(wv_ref[...], grad_pv[...])
    total[:, own] += dot_nn(wq_ref[...], grad_pq[...])
    for frame in range(FRAMES):
        gt_ref[frame] = total[:, frame * ROWS : (frame + 1) * ROWS].astype(jnp.bfloat16)
        for pair in range(PAIRS):
            lanes = slice(pair * 128, pair * 128 + 128)
            dv_ref[frame, :, lanes] = dot_nt(
                weight_ref[frame, pair].astype(jnp.bfloat16), split_heads(gt_ref[frame, lanes, :])
            ).astype(jnp.bfloat16)


def pool_frames(frame_now, weights, values, w_query, w_key, w_value, upstream_t):
    wide = (WIDTH, FRAMES * ROWS)
    return pl.pallas_call(
        pool_kernel,
        out_shape=(
            jax.ShapeDtypeStruct((WIDTH, ROWS), jnp.bfloat16),
            jax.ShapeDtypeStruct((FRAMES, WIDTH, ROWS), jnp.bfloat16),
            jax.ShapeDtypeStruct((FRAMES, ROWS, WIDTH), jnp.bfloat16),
        ),
        in_specs=[smem()] + [vmem()] * 9,
        out_specs=(vmem(), vmem(), vmem()),
        scratch_shapes=[
            pltpu.VMEM(wide, jnp.bfloat16),
            pltpu.VMEM(wide, jnp.float32),
            pltpu.VMEM(wide, jnp.float32),
            pltpu.VMEM((WIDTH, ROWS), jnp.float32),
            pltpu.VMEM(wide, jnp.bfloat16),
            pltpu.VMEM(wide, jnp.bfloat16),
            pltpu.VMEM((WIDTH, ROWS), jnp.bfloat16),
            pltpu.VMEM(wide, jnp.float32),
        ],
        compiler_params=params(),
        name="pool_frames",
    )(
        frame_now.reshape(1),
        weights,
        values,
        w_query,
        w_key,
        w_value,
        w_query.T,
        w_key.T,
        w_value.T,
        upstream_t,
    )


def back_kernel(query_ref, key_ref, value_ref, weight_ref, gt_ref, gq_ref, dk_ref, total):
    frame = pl.program_id(0)

    @pl.when(frame == 0)
    def _():
        total[...] = jnp.zeros_like(total)

    for pair in range(PAIRS):
        lanes = slice(pair * 128, pair * 128 + 128)
        weight = weight_ref[0, pair]
        grad_w = dot_nn(value_ref[0, :, lanes], split_heads(gt_ref[0, lanes, :]))
        inner = jnp.sum(weight * grad_w, axis=0, keepdims=True)
        grad_s = (weight * (grad_w - inner) * SCALE).astype(jnp.bfloat16)
        dk_ref[0, :, lanes] = dot_nt(grad_s, split_heads(query_ref[lanes, :])).astype(jnp.bfloat16)
        total[lanes, :] += join_heads(dot_tn(key_ref[0, :, lanes], grad_s))

    @pl.when(frame == FRAMES - 1)
    def _():
        gq_ref[...] = total[...].astype(jnp.bfloat16)


def attend_back(query_t, keys, values, weights, grad_traj):
    by_frame = pl.BlockSpec((1, ROWS, WIDTH), lambda f: (f, 0, 0))
    whole = pl.BlockSpec((WIDTH, ROWS), lambda f: (0, 0))
    return pl.pallas_call(
        back_kernel,
        grid=(FRAMES,),
        out_shape=(
            jax.ShapeDtypeStruct((WIDTH, ROWS), jnp.bfloat16),
            jax.ShapeDtypeStruct((FRAMES, ROWS, WIDTH), jnp.bfloat16),
        ),
        in_specs=[
            whole,
            by_frame,
            by_frame,
            pl.BlockSpec((1, PAIRS, ROWS, 2 * ROWS), lambda f: (f, 0, 0, 0)),
            pl.BlockSpec((1, WIDTH, ROWS), lambda f: (f, 0, 0)),
        ],
        out_specs=(whole, by_frame),
        scratch_shapes=[pltpu.VMEM((WIDTH, ROWS), jnp.float32)],
        compiler_params=params(),
        name="attend_back",
    )(query_t, keys, values, weights, grad_traj)


def merge_kernel(place_ref, mine_ref, theirs_ref, *refs):
    outs, acc = refs[:5], refs[5]
    acc[...] = jnp.zeros_like(acc)
    for source, ref in enumerate((mine_ref, theirs_ref)):

        @pl.loop(0, FRAMES * SLOTS)
        def _(slot):
            place = place_ref[source * FRAMES * SLOTS + slot]

            @pl.when(place >= 0)
            def _():
                acc[place] += ref[slot].astype(jnp.float32)

    at = 0
    for out in outs:
        size = out.shape[0]
        out[...] = acc[at : at + size].astype(jnp.bfloat16)
        at += size


def merge_slots(places, mine, theirs):
    sizes = (8, 8, 4, 4, 8)
    return pl.pallas_call(
        merge_kernel,
        out_shape=tuple(jax.ShapeDtypeStruct((n, TILE, WIDTH), jnp.bfloat16) for n in sizes),
        in_specs=[smem(), vmem(), vmem()],
        out_specs=(vmem(),) * 5,
        scratch_shapes=[pltpu.VMEM((32, TILE, WIDTH), jnp.float32)],
        compiler_params=params(),
        name="merge_slots",
    )(places, mine, theirs)


def add_wide(*terms):
    total = terms[0].astype(jnp.float32)
    for term in terms[1:]:
        total = total + term.astype(jnp.float32)
    return total.astype(jnp.bfloat16)


def scatter_frame(places, slot_grads):
    mine = lax.all_to_all(slot_grads, TM, split_axis=0, concat_axis=0, tiled=True)
    mine = mine.reshape(FRAMES * SLOTS, TILE, WIDTH)
    theirs = shift(mine, "c", 1)
    to_right, to_left, keep_right, keep_left, own = merge_slots(places, mine, theirs)
    from_left = shift(to_right, "x", 1)
    from_right = shift(to_left, "x", -1)
    low = shift(add_wide(keep_right, from_left[0:4]), "x", 1)
    high = shift(add_wide(keep_left, from_right[0:4]), "x", -1)
    first = add_wide(own[0:4], from_right[4:8], low)
    second = add_wide(own[4:8], from_left[4:8], high)
    up = jnp.concatenate([second[0:1], first[3:4]], axis=0)
    down = jnp.concatenate([second[1:2], second[2:3]], axis=0)
    from_down = shift(up, "zh", 1)
    from_up = shift(down, "zh", -1)
    tile_low = shift(add_wide(first[2:3], from_down[0:1]), "zh", 1)
    tile_high = shift(add_wide(second[3:4], from_up[0:1]), "zh", -1)
    return jnp.concatenate(
        [
            add_wide(first[0:1], from_up[1:2], tile_low),
            add_wide(first[1:2], from_down[1:2], tile_high),
        ],
        axis=0,
    )


def per_device(queries, keys, values, w_query, w_key, w_value, grad_out, tile_list, tile_count):
    frame_now = lax.axis_index("y") * 2 + lax.axis_index("zl")
    at_z, at_x, at_c = (lax.axis_index(a) for a in SPACE)
    my_space = (at_z * 4 + at_x) * 2 + at_c
    pair_space = (at_z * 4 + at_x) * 2

    wanted = lax.dynamic_slice(
        tile_list, (0, pair_space, frame_now, 0), (FRAMES, 2, 1, SLOTS)
    ).reshape(FRAMES, 2, SLOTS)
    wanted = wanted.transpose(1, 0, 2).reshape(2, FRAMES * SLOTS)
    mine_wanted = lax.dynamic_index_in_dim(wanted, at_c, 0, keepdims=False)
    their_wanted = lax.dynamic_index_in_dim(wanted, 1 - at_c, 0, keepdims=False)

    def locate(tiles):
        owner = tiles // 2
        z_rel = (owner // 8 - at_z) % 4
        x_rel = (owner // 2 % 4 - at_x) % 4
        other = (owner % 2 != at_c).astype(jnp.int32)
        return z_rel * 2 + tiles % 2, x_rel, other

    inside, x_rel, other = locate(mine_wanted)
    high = (inside >= 4).astype(jnp.int32)
    piece = jnp.where(x_rel < 2, x_rel, jnp.where(x_rel == 3, 4, 2 + high))
    piece_ids = piece + 5 * other
    piece_rows = jnp.where(x_rel == 2, inside - 4 * high, inside)

    def placing(tiles):
        inside, x_rel, other = locate(tiles)
        high = inside >= 4
        low_part = inside % 4
        place = jnp.where(
            x_rel == 0,
            24 + inside,
            jnp.where(
                x_rel == 1,
                jnp.where(high, 4 + low_part, 16 + low_part),
                jnp.where(
                    x_rel == 2,
                    jnp.where(high, 8 + low_part, low_part),
                    jnp.where(high, 20 + low_part, 12 + low_part),
                ),
            ),
        )
        return jnp.where(other == 1, -1, place)

    places = jnp.concatenate([placing(mine_wanted), placing(their_wanted)])

    def fetch(own):
        pieces = gather_frame(own.reshape(2, TILE, WIDTH))
        chosen = select_tiles(piece_ids, piece_rows, pieces)
        got = lax.all_to_all(
            chosen.reshape(FRAMES, SLOTS * TILE, WIDTH), TM, split_axis=0, concat_axis=0, tiled=True
        )
        return got

    counts = lax.dynamic_slice(tile_count, (frame_now, my_space, 0), (1, 1, FRAMES)).reshape(FRAMES)
    query_t = queries.reshape(ROWS, WIDTH).T
    upstream_t = grad_out.reshape(ROWS, WIDTH).T
    key_slots = fetch(keys)
    value_slots = fetch(values)
    weights = attend_weights(counts, query_t, key_slots)
    mixed_t, grad_traj, slot_dv = pool_frames(
        frame_now, weights, value_slots, w_query, w_key, w_value, upstream_t
    )
    grad_query_t, slot_dk = attend_back(query_t, key_slots, value_slots, weights, grad_traj)
    sum_values = scatter_frame(places, slot_dv)
    sum_keys = scatter_frame(places, slot_dk)
    shape = (1, ROWS, WIDTH)
    return (
        mixed_t.T.reshape(shape),
        grad_query_t.T.reshape(shape),
        sum_keys.reshape(shape),
        sum_values.reshape(shape),
    )


def solution(mesh):
    fine = Mesh(mesh.devices.reshape(4, 2, 4, 4, 2), TM + SPACE)
    rows = P(TM, SPACE, None)
    return jax.shard_map(
        per_device,
        mesh=fine,
        in_specs=(rows, rows, rows, P(), P(), P(), rows, P(), P()),
        out_specs=(rows, rows, rows, rows),
        check_vma=False,
    )
```

```python
import functools

import jax
import jax.numpy as jnp
from jax import lax
from jax.experimental import pallas as pl
from jax.experimental.pallas import tpu as pltpu
from jax.sharding import Mesh
from jax.sharding import PartitionSpec as P

HEAD = 64
HEADS = 8
TILE = 64
FRAMES = 8
SLOTS = 2
WIDTH = 512
PAIRS = 4
ROWS = 128
SCALE = 0.125
PIECES = 8
TM = ("y", "zl")
SPACE = ("zh", "x", "c")
VMEM_LIMIT = 56 * 1024 * 1024


def params():
    return pltpu.CompilerParams(vmem_limit_bytes=VMEM_LIMIT)


def whole():
    return pl.BlockSpec()


def smem():
    return pl.BlockSpec(memory_space=pltpu.SMEM)


def hbm():
    return pl.BlockSpec(memory_space=pl.ANY)


def shift(value, axis, step):
    size = lax.axis_size(axis)
    return lax.ppermute(value, axis, [(i, (i + step) % size) for i in range(size)])


def after(value, *others):
    return lax.optimization_barrier((value,) + others)[0]


def swap(pieces):
    return [shift(piece, "c", 1) for piece in pieces]


def spread(value, axis):
    far = shift(value, axis, 2)
    return [shift(value, axis, -1), far, shift(value, axis, 1)]


def gather_frames(keys, values):
    column_k = jnp.concatenate([keys] + spread(keys, "zh"), axis=0)
    column_v = jnp.concatenate([values] + spread(values, "zh"), axis=0)
    rows_k = spread(column_k, "x")
    rows_v = spread(column_v, "x")
    rows_k = lax.optimization_barrier(tuple(rows_k) + (column_v,))[:3]
    pieces_k = [column_k, *rows_k]
    pieces_v = [column_v, *rows_v]
    return pieces_k + swap(pieces_k), pieces_v + swap(pieces_v), rows_v[1]


def select_kernel(piece_ref, row_ref, *refs):
    pieces, out_ref, sems = refs[:PIECES], refs[PIECES], refs[PIECES + 1]

    @pl.loop(0, FRAMES * SLOTS)
    def _(slot):
        which = piece_ref[slot]
        row = row_ref[slot]
        for number, piece in enumerate(pieces):

            @pl.when(which == number)
            def _():
                pltpu.make_async_copy(
                    piece.at[pl.ds(row, 1)], out_ref.at[pl.ds(slot, 1)], sems.at[slot]
                ).start()

    @pl.loop(0, FRAMES * SLOTS)
    def _(slot):
        pltpu.make_async_copy(
            pieces[0].at[pl.ds(0, 1)], out_ref.at[pl.ds(slot, 1)], sems.at[slot]
        ).wait()


def select_tiles(piece_ids, piece_rows, pieces):
    return pl.pallas_call(
        select_kernel,
        out_shape=jax.ShapeDtypeStruct((FRAMES * SLOTS, TILE, WIDTH), jnp.bfloat16),
        in_specs=[smem(), smem()] + [hbm()] * PIECES,
        out_specs=whole(),
        scratch_shapes=[pltpu.SemaphoreType.DMA((FRAMES * SLOTS,))],
        compiler_params=params(),
        name="select_tiles",
    )(piece_ids, piece_rows, *pieces)


def split_heads(pair):
    rows = lax.broadcasted_iota(jnp.int32, pair.shape, 0)
    zero = jnp.zeros_like(pair)
    return jnp.concatenate(
        [jnp.where(rows < HEAD, pair, zero), jnp.where(rows >= HEAD, pair, zero)], axis=1
    )


def join_heads(both):
    return jnp.concatenate([both[:HEAD, :ROWS], both[HEAD:, ROWS:]], axis=0)


def dot_nn(a, b):
    return jnp.dot(a, b, preferred_element_type=jnp.float32)


def dot_tn(a, b):
    return lax.dot_general(a, b, (((0,), (0,)), ((), ())), preferred_element_type=jnp.float32)


def dot_nt(a, b):
    return lax.dot_general(a, b, (((1,), (1,)), ((), ())), preferred_element_type=jnp.float32)


def weights_kernel(count_ref, query_ref, key_ref, weight_ref, narrow_ref):
    frame = pl.program_id(0)
    limit = count_ref[frame] * TILE
    rows = lax.broadcasted_iota(jnp.int32, (ROWS, 2 * ROWS), 0)
    live = rows < limit
    for pair in range(PAIRS):
        lanes = slice(pair * 128, pair * 128 + 128)
        scores = dot_nn(key_ref[0, :, lanes], split_heads(query_ref[lanes, :])) * SCALE
        scores = jnp.where(live, scores, -jnp.inf)
        raised = jnp.exp(scores - jnp.max(scores, axis=0, keepdims=True))
        weights = raised / jnp.sum(raised, axis=0, keepdims=True)
        weight_ref[0, pair] = weights
        narrow_ref[0, pair] = weights.astype(jnp.bfloat16)


def attend_weights(counts, query_t, keys):
    return pl.pallas_call(
        weights_kernel,
        grid=(FRAMES,),
        out_shape=(
            jax.ShapeDtypeStruct((FRAMES, PAIRS, ROWS, 2 * ROWS), jnp.float32),
            jax.ShapeDtypeStruct((FRAMES, PAIRS, ROWS, 2 * ROWS), jnp.bfloat16),
        ),
        in_specs=[
            smem(),
            pl.BlockSpec((WIDTH, ROWS), lambda f: (0, 0)),
            pl.BlockSpec((1, ROWS, WIDTH), lambda f: (f, 0, 0)),
        ],
        out_specs=(pl.BlockSpec((1, PAIRS, ROWS, 2 * ROWS), lambda f: (f, 0, 0, 0)),) * 2,
        compiler_params=params(),
        name="attend_weights",
    )(counts, query_t, keys)


def pool_kernel(
    frame_ref,
    weight_ref,
    value_ref,
    wq_ref,
    wk_ref,
    wv_ref,
    wqt_ref,
    wkt_ref,
    wvt_ref,
    go_ref,
    mixed_ref,
    gt_ref,
    dv_ref,
    traj,
    pooled_k,
    pooled_v,
    pooled_q,
    grad_pk,
    grad_pv,
    grad_pq,
    total,
):
    for frame in range(FRAMES):
        for pair in range(PAIRS):
            lanes = slice(pair * 128, pair * 128 + 128)
            both = dot_tn(value_ref[frame, :, lanes], weight_ref[frame, pair])
            traj[lanes, frame * ROWS : (frame + 1) * ROWS] = join_heads(both).astype(jnp.bfloat16)
    own = pl.ds(pl.multiple_of(frame_ref[0] * ROWS, ROWS), ROWS)
    pooled_q[...] = dot_nn(wqt_ref[...], traj[:, own])
    pooled_k[...] = dot_nn(wkt_ref[...], traj[...])
    pooled_v[...] = dot_nn(wvt_ref[...], traj[...])
    for head in range(HEADS):
        rows = slice(head * HEAD, (head + 1) * HEAD)
        query = pooled_q[rows, :]
        upstream = go_ref[rows, :].astype(jnp.float32)
        columns = [slice(f * ROWS, (f + 1) * ROWS) for f in range(FRAMES)]
        logits = jnp.concatenate(
            [
                jnp.sum(query * pooled_k[rows, columns[f]], axis=0, keepdims=True)
                for f in range(FRAMES)
            ],
            axis=0,
        )
        raised = jnp.exp(logits * SCALE)
        fw = raised / jnp.sum(raised, axis=0, keepdims=True)
        grad_fw = jnp.concatenate(
            [
                jnp.sum(upstream * pooled_v[rows, columns[f]], axis=0, keepdims=True)
                for f in range(FRAMES)
            ],
            axis=0,
        )
        inner = jnp.sum(fw * grad_fw, axis=0, keepdims=True)
        grad_logit = fw * (grad_fw - inner) * SCALE
        mixed = jnp.zeros((HEAD, ROWS), jnp.float32)
        grad_query = jnp.zeros((HEAD, ROWS), jnp.float32)
        for f in range(FRAMES):
            weight = fw[f : f + 1, :]
            slope = grad_logit[f : f + 1, :]
            mixed = mixed + weight * pooled_v[rows, columns[f]]
            grad_query = grad_query + slope * pooled_k[rows, columns[f]]
            grad_pk[rows, columns[f]] = (slope * query).astype(jnp.bfloat16)
            grad_pv[rows, columns[f]] = (weight * upstream).astype(jnp.bfloat16)
        pooled_q[rows, :] = mixed
        grad_pq[rows, :] = grad_query.astype(jnp.bfloat16)
    mixed_ref[...] = pooled_q[...].T.astype(jnp.bfloat16)
    total[...] = dot_nn(wk_ref[...], grad_pk[...]) + dot_nn(wv_ref[...], grad_pv[...])
    total[:, own] += dot_nn(wq_ref[...], grad_pq[...])
    for frame in range(FRAMES):
        gt_ref[frame] = total[:, frame * ROWS : (frame + 1) * ROWS].astype(jnp.bfloat16)
        for pair in range(PAIRS):
            lanes = slice(pair * 128, pair * 128 + 128)
            dv_ref[frame, :, lanes] = dot_nt(
                weight_ref[frame, pair], split_heads(gt_ref[frame, lanes, :])
            ).astype(jnp.bfloat16)


def pool_frames(frame_now, weights, values, w_query, w_key, w_value, upstream_t):
    wide = (WIDTH, FRAMES * ROWS)
    return pl.pallas_call(
        pool_kernel,
        out_shape=(
            jax.ShapeDtypeStruct((ROWS, WIDTH), jnp.bfloat16),
            jax.ShapeDtypeStruct((FRAMES, WIDTH, ROWS), jnp.bfloat16),
            jax.ShapeDtypeStruct((FRAMES, ROWS, WIDTH), jnp.bfloat16),
        ),
        in_specs=[smem()] + [whole()] * 9,
        out_specs=(whole(), whole(), whole()),
        scratch_shapes=[
            pltpu.VMEM(wide, jnp.bfloat16),
            pltpu.VMEM(wide, jnp.float32),
            pltpu.VMEM(wide, jnp.float32),
            pltpu.VMEM((WIDTH, ROWS), jnp.float32),
            pltpu.VMEM(wide, jnp.bfloat16),
            pltpu.VMEM(wide, jnp.bfloat16),
            pltpu.VMEM((WIDTH, ROWS), jnp.bfloat16),
            pltpu.VMEM(wide, jnp.float32),
        ],
        compiler_params=params(),
        name="pool_frames",
    )(
        frame_now.reshape(1),
        weights,
        values,
        w_query,
        w_key,
        w_value,
        w_query.T,
        w_key.T,
        w_value.T,
        upstream_t,
    )


def back_kernel(query_ref, key_ref, value_ref, weight_ref, gt_ref, gq_ref, dk_ref, total):
    frame = pl.program_id(0)

    @pl.when(frame == 0)
    def _():
        total[...] = jnp.zeros_like(total)

    for pair in range(PAIRS):
        lanes = slice(pair * 128, pair * 128 + 128)
        weight = weight_ref[0, pair]
        grad_w = dot_nn(value_ref[0, :, lanes], split_heads(gt_ref[0, lanes, :]))
        inner = jnp.sum(weight * grad_w, axis=0, keepdims=True)
        grad_s = (weight * (grad_w - inner) * SCALE).astype(jnp.bfloat16)
        dk_ref[0, :, lanes] = dot_nt(grad_s, split_heads(query_ref[lanes, :])).astype(jnp.bfloat16)
        total[lanes, :] += join_heads(dot_tn(key_ref[0, :, lanes], grad_s))

    @pl.when(frame == FRAMES - 1)
    def _():
        gq_ref[...] = total[...].T.astype(jnp.bfloat16)


def attend_back(query_t, keys, values, weights, grad_traj):
    by_frame = pl.BlockSpec((1, ROWS, WIDTH), lambda f: (f, 0, 0))
    fixed = pl.BlockSpec((WIDTH, ROWS), lambda f: (0, 0))
    return pl.pallas_call(
        back_kernel,
        grid=(FRAMES,),
        out_shape=(
            jax.ShapeDtypeStruct((ROWS, WIDTH), jnp.bfloat16),
            jax.ShapeDtypeStruct((FRAMES, ROWS, WIDTH), jnp.bfloat16),
        ),
        in_specs=[
            fixed,
            by_frame,
            by_frame,
            pl.BlockSpec((1, PAIRS, ROWS, 2 * ROWS), lambda f: (f, 0, 0, 0)),
            pl.BlockSpec((1, WIDTH, ROWS), lambda f: (f, 0, 0)),
        ],
        out_specs=(pl.BlockSpec((ROWS, WIDTH), lambda f: (0, 0)), by_frame),
        scratch_shapes=[pltpu.VMEM((WIDTH, ROWS), jnp.float32)],
        compiler_params=params(),
        name="attend_back",
    )(query_t, keys, values, weights, grad_traj)


def merge_kernel(place_ref, mine_ref, theirs_ref, *refs):
    outs, acc = refs[:5], refs[5]
    acc[...] = jnp.zeros_like(acc)
    for source, ref in enumerate((mine_ref, theirs_ref)):

        @pl.loop(0, FRAMES * SLOTS)
        def _(slot):
            place = place_ref[source * FRAMES * SLOTS + slot]

            @pl.when(place >= 0)
            def _():
                acc[place] += ref[slot].astype(jnp.float32)

    at = 0
    for out in outs:
        size = out.shape[0]
        out[...] = acc[at : at + size].astype(jnp.bfloat16)
        at += size


def merge_slots(places, mine, theirs):
    sizes = (8, 8, 4, 4, 8)
    return pl.pallas_call(
        merge_kernel,
        out_shape=tuple(jax.ShapeDtypeStruct((n, TILE, WIDTH), jnp.bfloat16) for n in sizes),
        in_specs=[smem(), whole(), whole()],
        out_specs=(whole(),) * 5,
        scratch_shapes=[pltpu.VMEM((32, TILE, WIDTH), jnp.float32)],
        compiler_params=params(),
        name="merge_slots",
    )(places, mine, theirs)


def add_wide(*terms):
    total = terms[0].astype(jnp.float32)
    for term in terms[1:]:
        total = total + term.astype(jnp.float32)
    return total.astype(jnp.bfloat16)


def scatter_rows(merged):
    to_right, to_left, keep_right, keep_left, own = merged
    from_left = shift(to_right, "x", 1)
    from_right = shift(to_left, "x", -1)
    return keep_right, keep_left, own, from_left, from_right


def scatter_across(state):
    keep_right, keep_left, own, from_left, from_right = state
    low = shift(add_wide(keep_right, from_left[0:4]), "x", 1)
    high = shift(add_wide(keep_left, from_right[0:4]), "x", -1)
    return own, from_left, from_right, low, high


def scatter_column(state):
    own, from_left, from_right, low, high = state
    here = add_wide(own[0:2], from_right[4:6], low[0:2])
    up = add_wide(own[2:4], from_right[6:8], low[2:4])
    far = add_wide(own[4:6], from_left[4:6], high[0:2])
    down = add_wide(own[6:8], from_left[6:8], high[2:4])
    return add_wide(here, shift(up, "zh", 1), shift(far, "zh", 2), shift(down, "zh", -1))


def per_device(queries, keys, values, w_query, w_key, w_value, grad_out, tile_list, tile_count):
    frame_now = lax.axis_index("y") * 2 + lax.axis_index("zl")
    at_z, at_x, at_c = (lax.axis_index(a) for a in SPACE)
    my_space = (at_z * 4 + at_x) * 2 + at_c
    pair_space = (at_z * 4 + at_x) * 2

    wanted = lax.dynamic_slice(
        tile_list, (0, pair_space, frame_now, 0), (FRAMES, 2, 1, SLOTS)
    ).reshape(FRAMES, 2, SLOTS)
    wanted = wanted.transpose(1, 0, 2).reshape(2, FRAMES * SLOTS)
    mine_wanted = lax.dynamic_index_in_dim(wanted, at_c, 0, keepdims=False)
    their_wanted = lax.dynamic_index_in_dim(wanted, 1 - at_c, 0, keepdims=False)

    def locate(tiles):
        owner = tiles // 2
        z_rel = (owner // 8 - at_z) % 4
        x_rel = (owner // 2 % 4 - at_x) % 4
        other = (owner % 2 != at_c).astype(jnp.int32)
        return z_rel * 2 + tiles % 2, x_rel, other

    inside, x_rel, other = locate(mine_wanted)
    piece_ids = x_rel + 4 * other

    def placing(tiles):
        inside, x_rel, other = locate(tiles)
        high = inside >= 4
        low_part = inside % 4
        place = jnp.where(
            x_rel == 0,
            24 + inside,
            jnp.where(
                x_rel == 1,
                jnp.where(high, 4 + low_part, 16 + low_part),
                jnp.where(
                    x_rel == 2,
                    jnp.where(high, 8 + low_part, low_part),
                    jnp.where(high, 20 + low_part, 12 + low_part),
                ),
            ),
        )
        return jnp.where(other == 1, -1, place)

    places = jnp.concatenate([placing(mine_wanted), placing(their_wanted)])

    def exchange(chosen):
        return lax.all_to_all(
            chosen.reshape(FRAMES, SLOTS * TILE, WIDTH), TM, split_axis=0, concat_axis=0, tiled=True
        )

    counts = lax.dynamic_slice(tile_count, (frame_now, my_space, 0), (1, 1, FRAMES)).reshape(FRAMES)
    query_t = queries.reshape(ROWS, WIDTH).T
    upstream_t = grad_out.reshape(ROWS, WIDTH).T
    own_shape = (2, TILE, WIDTH)
    key_pieces, value_pieces, far_v = gather_frames(keys.reshape(own_shape), values.reshape(own_shape))
    key_slots = exchange(after(select_tiles(piece_ids, inside, key_pieces), far_v))
    value_slots = exchange(select_tiles(piece_ids, inside, value_pieces))
    weights, narrow = attend_weights(counts, query_t, key_slots)
    mixed, grad_traj, slot_dv = pool_frames(
        frame_now, narrow, value_slots, w_query, w_key, w_value, upstream_t
    )
    grad_queries, slot_dk = attend_back(query_t, key_slots, value_slots, weights, grad_traj)
    owned_v = exchange(slot_dv).reshape(FRAMES * SLOTS, TILE, WIDTH)
    merged_v = merge_slots(places, owned_v, shift(owned_v, "c", 1))
    owned_k = exchange(slot_dk).reshape(FRAMES * SLOTS, TILE, WIDTH)
    owned_k = after(owned_k, *merged_v)
    state_v = scatter_rows(merged_v)
    merged_k = merge_slots(places, owned_k, shift(owned_k, "c", 1))
    state_k = scatter_rows(merged_k)
    state_v = lax.optimization_barrier(state_v + (merged_k[0],))[:5]
    state_v = scatter_across(state_v)
    state_k = scatter_across(state_k)
    sum_values = scatter_column(state_v)
    sum_keys = scatter_column(state_k)
    shape = (1, ROWS, WIDTH)
    return (
        mixed.reshape(shape),
        grad_queries.reshape(shape),
        sum_keys.reshape(shape),
        sum_values.reshape(shape),
    )


def solution(mesh):
    fine = Mesh(mesh.devices.reshape(4, 2, 4, 4, 2), TM + SPACE)
    rows = P(TM, SPACE, None)
    return jax.shard_map(
        per_device,
        mesh=fine,
        in_specs=(rows, rows, rows, P(), P(), P(), rows, P(), P()),
        out_specs=(rows, rows, rows, rows),
        check_vma=False,
    )
```

```python
import functools

import jax
import jax.numpy as jnp
from jax import lax
from jax.experimental import pallas as pl
from jax.experimental.pallas import tpu as pltpu
from jax.sharding import Mesh
from jax.sharding import PartitionSpec as P

HEAD = 64
HEADS = 8
TILE = 64
FRAMES = 8
SLOTS = 2
WIDTH = 512
PAIRS = 4
ROWS = 128
SCALE = 0.125
TM = ("y", "zl")
SPACE = ("zh", "x", "c")
VMEM_LIMIT = 63 * 1024 * 1024


def params(size=VMEM_LIMIT):
    return pltpu.CompilerParams(vmem_limit_bytes=size)


def cost(micros):
    return pl.CostEstimate(flops=micros * 1000000000, bytes_accessed=0, transcendentals=0)


def whole():
    return pl.BlockSpec()


def smem():
    return pl.BlockSpec(memory_space=pltpu.SMEM)


def hbm():
    return pl.BlockSpec(memory_space=pl.ANY)


def shift(value, axis, step):
    size = lax.axis_size(axis)
    return lax.ppermute(value, axis, [(i, (i + step) % size) for i in range(size)])


def after(value, *others):
    return lax.optimization_barrier((value,) + others)[0]


def swap(pieces):
    return [shift(piece, "c", 1) for piece in pieces]


def spread(value, axis):
    far = shift(value, axis, 2)
    return [shift(value, axis, -1), far, shift(value, axis, 1)]


def gather_frames(keys, values):
    column_k = jnp.concatenate([keys] + spread(keys, "zh"), axis=0)
    column_v = jnp.concatenate([values] + spread(values, "zh"), axis=0)
    rows_k = spread(column_k, "x")
    rows_v = spread(column_v, "x")
    rows_k = lax.optimization_barrier(tuple(rows_k) + (column_v,))[:3]
    pieces_k = [column_k, *rows_k]
    pieces_v = [column_v, *rows_v]
    return pieces_k + swap(pieces_k), pieces_v + swap(pieces_v)


def select_kernel(piece_ref, row_ref, *refs):
    pieces, out_ref, sems = refs[:-2], refs[-2], refs[-1]

    @pl.loop(0, FRAMES * SLOTS)
    def _(slot):
        which = piece_ref[slot]
        row = row_ref[slot]
        for number, piece in enumerate(pieces):

            @pl.when(which == number)
            def _():
                pltpu.make_async_copy(
                    piece.at[pl.ds(row, 1)], out_ref.at[pl.ds(slot, 1)], sems.at[slot]
                ).start()

    @pl.loop(0, FRAMES * SLOTS)
    def _(slot):
        pltpu.make_async_copy(
            pieces[0].at[pl.ds(0, 1)], out_ref.at[pl.ds(slot, 1)], sems.at[slot]
        ).wait()


def select_tiles(piece_ids, piece_rows, pieces, micros=0):
    return pl.pallas_call(
        select_kernel,
        out_shape=jax.ShapeDtypeStruct((FRAMES * SLOTS, TILE, WIDTH), jnp.bfloat16),
        in_specs=[smem(), smem()] + [hbm()] * len(pieces),
        out_specs=whole(),
        scratch_shapes=[pltpu.SemaphoreType.DMA((FRAMES * SLOTS,))],
        compiler_params=params(6 * 1024 * 1024),
        cost_estimate=cost(micros),
        name="select_tiles",
    )(piece_ids, piece_rows, *pieces)


def split_heads(pair):
    rows = lax.broadcasted_iota(jnp.int32, pair.shape, 0)
    zero = jnp.zeros_like(pair)
    return jnp.concatenate(
        [jnp.where(rows < HEAD, pair, zero), jnp.where(rows >= HEAD, pair, zero)], axis=1
    )


def join_heads(both):
    return jnp.concatenate([both[:HEAD, :ROWS], both[HEAD:, ROWS:]], axis=0)


def dot_nn(a, b):
    return jnp.dot(a, b, preferred_element_type=jnp.float32)


def dot_tn(a, b):
    return lax.dot_general(a, b, (((0,), (0,)), ((), ())), preferred_element_type=jnp.float32)


def dot_nt(a, b):
    return lax.dot_general(a, b, (((1,), (1,)), ((), ())), preferred_element_type=jnp.float32)


def weights_kernel(count_ref, query_ref, key_ref, weight_ref, narrow_ref, turned):
    frame = pl.program_id(0)

    @pl.when(frame == 0)
    def _():
        turned[...] = query_ref[...].T

    limit = count_ref[frame] * TILE
    rows = lax.broadcasted_iota(jnp.int32, (ROWS, 2 * ROWS), 0)
    live = rows < limit
    for pair in range(PAIRS):
        lanes = slice(pair * 128, pair * 128 + 128)
        scores = dot_nn(key_ref[0, :, lanes], split_heads(turned[lanes, :])) * SCALE
        scores = jnp.where(live, scores, -jnp.inf)
        raised = jnp.exp(scores - jnp.max(scores, axis=0, keepdims=True))
        weights = raised / jnp.sum(raised, axis=0, keepdims=True)
        weight_ref[0, pair] = weights
        narrow_ref[0, pair] = weights.astype(jnp.bfloat16)


def attend_weights(counts, queries, keys):
    return pl.pallas_call(
        weights_kernel,
        grid=(FRAMES,),
        out_shape=(
            jax.ShapeDtypeStruct((FRAMES, PAIRS, ROWS, 2 * ROWS), jnp.float32),
            jax.ShapeDtypeStruct((FRAMES, PAIRS, ROWS, 2 * ROWS), jnp.bfloat16),
        ),
        in_specs=[
            smem(),
            pl.BlockSpec((ROWS, WIDTH), lambda f: (0, 0)),
            pl.BlockSpec((1, ROWS, WIDTH), lambda f: (f, 0, 0)),
        ],
        out_specs=(pl.BlockSpec((1, PAIRS, ROWS, 2 * ROWS), lambda f: (f, 0, 0, 0)),) * 2,
        scratch_shapes=[pltpu.VMEM((WIDTH, ROWS), jnp.bfloat16)],
        compiler_params=params(),
        name="attend_weights",
    )(counts, queries, keys)


def pool_kernel(
    frame_ref,
    weight_ref,
    value_ref,
    wq_ref,
    wk_ref,
    wv_ref,
    go_ref,
    mixed_ref,
    gt_ref,
    dv_ref,
    traj,
    pooled_k,
    pooled_v,
    pooled_q,
    grad_pk,
    grad_pv,
    grad_pq,
    total,
):
    for frame in range(FRAMES):
        for pair in range(PAIRS):
            lanes = slice(pair * 128, pair * 128 + 128)
            both = dot_tn(value_ref[frame, :, lanes], weight_ref[frame, pair])
            traj[lanes, frame * ROWS : (frame + 1) * ROWS] = join_heads(both).astype(jnp.bfloat16)
    own = pl.ds(pl.multiple_of(frame_ref[0] * ROWS, ROWS), ROWS)
    pooled_q[...] = dot_tn(wq_ref[...], traj[:, own])
    pooled_k[...] = dot_tn(wk_ref[...], traj[...])
    pooled_v[...] = dot_tn(wv_ref[...], traj[...])
    upstream_t = go_ref[...].astype(jnp.float32).T
    for head in range(HEADS):
        rows = slice(head * HEAD, (head + 1) * HEAD)
        query = pooled_q[rows, :]
        upstream = upstream_t[rows, :]
        columns = [slice(f * ROWS, (f + 1) * ROWS) for f in range(FRAMES)]
        logits = jnp.concatenate(
            [
                jnp.sum(query * pooled_k[rows, columns[f]], axis=0, keepdims=True)
                for f in range(FRAMES)
            ],
            axis=0,
        )
        raised = jnp.exp(logits * SCALE)
        fw = raised / jnp.sum(raised, axis=0, keepdims=True)
        grad_fw = jnp.concatenate(
            [
                jnp.sum(upstream * pooled_v[rows, columns[f]], axis=0, keepdims=True)
                for f in range(FRAMES)
            ],
            axis=0,
        )
        inner = jnp.sum(fw * grad_fw, axis=0, keepdims=True)
        grad_logit = fw * (grad_fw - inner) * SCALE
        mixed = jnp.zeros((HEAD, ROWS), jnp.float32)
        grad_query = jnp.zeros((HEAD, ROWS), jnp.float32)
        for f in range(FRAMES):
            weight = fw[f : f + 1, :]
            slope = grad_logit[f : f + 1, :]
            mixed = mixed + weight * pooled_v[rows, columns[f]]
            grad_query = grad_query + slope * pooled_k[rows, columns[f]]
            grad_pk[rows, columns[f]] = (slope * query).astype(jnp.bfloat16)
            grad_pv[rows, columns[f]] = (weight * upstream).astype(jnp.bfloat16)
        pooled_q[rows, :] = mixed
        grad_pq[rows, :] = grad_query.astype(jnp.bfloat16)
    mixed_ref[...] = pooled_q[...].T.astype(jnp.bfloat16)
    total[...] = dot_nn(wk_ref[...], grad_pk[...]) + dot_nn(wv_ref[...], grad_pv[...])
    total[:, own] += dot_nn(wq_ref[...], grad_pq[...])
    for frame in range(FRAMES):
        gt_ref[frame] = total[:, frame * ROWS : (frame + 1) * ROWS].astype(jnp.bfloat16)
        for pair in range(PAIRS):
            lanes = slice(pair * 128, pair * 128 + 128)
            dv_ref[frame, :, lanes] = dot_nt(
                weight_ref[frame, pair], split_heads(gt_ref[frame, lanes, :])
            ).astype(jnp.bfloat16)


def pool_frames(frame_now, weights, values, w_query, w_key, w_value, upstream):
    wide = (WIDTH, FRAMES * ROWS)
    return pl.pallas_call(
        pool_kernel,
        out_shape=(
            jax.ShapeDtypeStruct((ROWS, WIDTH), jnp.bfloat16),
            jax.ShapeDtypeStruct((FRAMES, WIDTH, ROWS), jnp.bfloat16),
            jax.ShapeDtypeStruct((FRAMES, ROWS, WIDTH), jnp.bfloat16),
        ),
        in_specs=[smem()] + [whole()] * 6,
        out_specs=(whole(), whole(), whole()),
        scratch_shapes=[
            pltpu.VMEM(wide, jnp.bfloat16),
            pltpu.VMEM(wide, jnp.float32),
            pltpu.VMEM(wide, jnp.float32),
            pltpu.VMEM((WIDTH, ROWS), jnp.float32),
            pltpu.VMEM(wide, jnp.bfloat16),
            pltpu.VMEM(wide, jnp.bfloat16),
            pltpu.VMEM((WIDTH, ROWS), jnp.bfloat16),
            pltpu.VMEM(wide, jnp.float32),
        ],
        compiler_params=params(),
        name="pool_frames",
    )(
        frame_now.reshape(1),
        weights,
        values,
        w_query,
        w_key,
        w_value,
        upstream,
    )


def back_kernel(query_ref, key_ref, value_ref, weight_ref, gt_ref, gq_ref, dk_ref, turned, total):
    frame = pl.program_id(0)

    @pl.when(frame == 0)
    def _():
        total[...] = jnp.zeros_like(total)
        turned[...] = query_ref[...].T

    for pair in range(PAIRS):
        lanes = slice(pair * 128, pair * 128 + 128)
        weight = weight_ref[0, pair]
        grad_w = dot_nn(value_ref[0, :, lanes], split_heads(gt_ref[0, lanes, :]))
        inner = jnp.sum(weight * grad_w, axis=0, keepdims=True)
        grad_s = (weight * (grad_w - inner) * SCALE).astype(jnp.bfloat16)
        dk_ref[0, :, lanes] = dot_nt(grad_s, split_heads(turned[lanes, :])).astype(jnp.bfloat16)
        total[lanes, :] += join_heads(dot_tn(key_ref[0, :, lanes], grad_s))

    @pl.when(frame == FRAMES - 1)
    def _():
        gq_ref[...] = total[...].T.astype(jnp.bfloat16)


def attend_back(queries, keys, values, weights, grad_traj):
    by_frame = pl.BlockSpec((1, ROWS, WIDTH), lambda f: (f, 0, 0))
    fixed = pl.BlockSpec((ROWS, WIDTH), lambda f: (0, 0))
    return pl.pallas_call(
        back_kernel,
        grid=(FRAMES,),
        out_shape=(
            jax.ShapeDtypeStruct((ROWS, WIDTH), jnp.bfloat16),
            jax.ShapeDtypeStruct((FRAMES, ROWS, WIDTH), jnp.bfloat16),
        ),
        in_specs=[
            fixed,
            by_frame,
            by_frame,
            pl.BlockSpec((1, PAIRS, ROWS, 2 * ROWS), lambda f: (f, 0, 0, 0)),
            pl.BlockSpec((1, WIDTH, ROWS), lambda f: (f, 0, 0)),
        ],
        out_specs=(fixed, by_frame),
        scratch_shapes=[
            pltpu.VMEM((WIDTH, ROWS), jnp.bfloat16),
            pltpu.VMEM((WIDTH, ROWS), jnp.float32),
        ],
        compiler_params=params(),
        name="attend_back",
    )(queries, keys, values, weights, grad_traj)


def merge_kernel(place_ref, mine_ref, theirs_ref, *refs):
    outs, acc = refs[:5], refs[5]
    acc[...] = jnp.zeros_like(acc)
    for source, ref in enumerate((mine_ref, theirs_ref)):

        @pl.loop(0, FRAMES * SLOTS)
        def _(slot):
            place = place_ref[source * FRAMES * SLOTS + slot]

            @pl.when(place >= 0)
            def _():
                acc[place] += ref[slot].astype(jnp.float32)

    at = 0
    for out in outs:
        size = out.shape[0]
        out[...] = acc[at : at + size].astype(jnp.bfloat16)
        at += size


def merge_slots(places, mine, theirs):
    sizes = (8, 8, 4, 4, 8)
    return pl.pallas_call(
        merge_kernel,
        out_shape=tuple(jax.ShapeDtypeStruct((n, TILE, WIDTH), jnp.bfloat16) for n in sizes),
        in_specs=[smem(), whole(), whole()],
        out_specs=(whole(),) * 5,
        scratch_shapes=[pltpu.VMEM((32, TILE, WIDTH), jnp.float32)],
        compiler_params=params(),
        name="merge_slots",
    )(places, mine, theirs)


def add_wide(*terms):
    total = terms[0].astype(jnp.float32)
    for term in terms[1:]:
        total = total + term.astype(jnp.float32)
    return total.astype(jnp.bfloat16)


def scatter_rows(merged):
    to_right, to_left, keep_right, keep_left, own = merged
    from_left = shift(to_right, "x", 1)
    from_right = shift(to_left, "x", -1)
    return keep_right, keep_left, own, from_left, from_right


def scatter_across(state):
    keep_right, keep_left, own, from_left, from_right = state
    low = shift(add_wide(keep_right, from_left[0:4]), "x", 1)
    high = shift(add_wide(keep_left, from_right[0:4]), "x", -1)
    return own, from_left, from_right, low, high


def scatter_column(state):
    own, from_left, from_right, low, high = state
    here = add_wide(own[0:2], from_right[4:6], low[0:2])
    up = add_wide(own[2:4], from_right[6:8], low[2:4])
    far = add_wide(own[4:6], from_left[4:6], high[0:2])
    down = add_wide(own[6:8], from_left[6:8], high[2:4])
    return add_wide(here, shift(up, "zh", 1), shift(far, "zh", 2), shift(down, "zh", -1))


def per_device(queries, keys, values, w_query, w_key, w_value, grad_out, tile_list, tile_count):
    frame_now = lax.axis_index("y") * 2 + lax.axis_index("zl")
    at_z, at_x, at_c = (lax.axis_index(a) for a in SPACE)
    my_space = (at_z * 4 + at_x) * 2 + at_c
    pair_space = (at_z * 4 + at_x) * 2

    wanted = lax.dynamic_slice(
        tile_list, (0, pair_space, frame_now, 0), (FRAMES, 2, 1, SLOTS)
    ).reshape(FRAMES, 2, SLOTS)
    wanted = wanted.transpose(1, 0, 2).reshape(2, FRAMES * SLOTS)
    mine_wanted = lax.dynamic_index_in_dim(wanted, at_c, 0, keepdims=False)
    their_wanted = lax.dynamic_index_in_dim(wanted, 1 - at_c, 0, keepdims=False)

    def locate(tiles):
        owner = tiles // 2
        z_rel = (owner // 8 - at_z) % 4
        x_rel = (owner // 2 % 4 - at_x) % 4
        other = (owner % 2 != at_c).astype(jnp.int32)
        return z_rel * 2 + tiles % 2, x_rel, other

    inside, x_rel, other = locate(mine_wanted)
    piece_ids = x_rel + 4 * other

    def placing(tiles):
        inside, x_rel, other = locate(tiles)
        high = inside >= 4
        low_part = inside % 4
        place = jnp.where(
            x_rel == 0,
            24 + inside,
            jnp.where(
                x_rel == 1,
                jnp.where(high, 4 + low_part, 16 + low_part),
                jnp.where(
                    x_rel == 2,
                    jnp.where(high, 8 + low_part, low_part),
                    jnp.where(high, 20 + low_part, 12 + low_part),
                ),
            ),
        )
        return jnp.where(other == 1, -1, place)

    places = jnp.concatenate([placing(mine_wanted), placing(their_wanted)])

    def exchange(chosen):
        return lax.all_to_all(
            chosen.reshape(FRAMES, SLOTS * TILE, WIDTH), TM, split_axis=0, concat_axis=0, tiled=True
        )

    counts = lax.dynamic_slice(tile_count, (frame_now, my_space, 0), (1, 1, FRAMES)).reshape(FRAMES)
    query_rows = queries.reshape(ROWS, WIDTH)
    upstream_rows = grad_out.reshape(ROWS, WIDTH)
    own_shape = (2, TILE, WIDTH)
    key_pieces, value_pieces = gather_frames(keys.reshape(own_shape), values.reshape(own_shape))
    key_slots = exchange(select_tiles(piece_ids, inside, key_pieces))
    value_slots = exchange(select_tiles(piece_ids, inside, value_pieces, 13))
    weights, narrow = attend_weights(counts, query_rows, key_slots)
    mixed, grad_traj, slot_dv = pool_frames(
        frame_now, narrow, value_slots, w_query, w_key, w_value, upstream_rows
    )
    grad_queries, slot_dk = attend_back(query_rows, key_slots, value_slots, weights, grad_traj)
    owned_v = exchange(slot_dv).reshape(FRAMES * SLOTS, TILE, WIDTH)
    owned_v = after(owned_v, slot_dk)
    merged_v = merge_slots(places, owned_v, shift(owned_v, "c", 1))
    owned_k = exchange(slot_dk).reshape(FRAMES * SLOTS, TILE, WIDTH)
    owned_k = after(owned_k, *merged_v)
    state_v = scatter_rows(merged_v)
    merged_k = merge_slots(places, owned_k, shift(owned_k, "c", 1))
    state_k = scatter_rows(merged_k)
    state_v = lax.optimization_barrier(state_v + (merged_k[0],))[:5]
    state_v = scatter_across(state_v)
    state_k = scatter_across(state_k)
    sum_values = scatter_column(state_v)
    sum_keys = scatter_column(state_k)
    shape = (1, ROWS, WIDTH)
    return (
        mixed.reshape(shape),
        grad_queries.reshape(shape),
        sum_keys.reshape(shape),
        sum_values.reshape(shape),
    )


def solution(mesh):
    fine = Mesh(mesh.devices.reshape(4, 2, 4, 4, 2), TM + SPACE)
    rows = P(TM, SPACE, None)
    return jax.shard_map(
        per_device,
        mesh=fine,
        in_specs=(rows, rows, rows, P(), P(), P(), rows, P(), P()),
        out_specs=(rows, rows, rows, rows),
        check_vma=False,
    )
```

```python
import functools

import jax
import jax.numpy as jnp
from jax import lax
from jax.experimental import pallas as pl
from jax.experimental.pallas import tpu as pltpu
from jax.sharding import Mesh
from jax.sharding import PartitionSpec as P

HEAD = 64
HEADS = 8
TILE = 64
FRAMES = 8
SLOTS = 2
WIDTH = 512
PAIRS = 4
ROWS = 128
SCALE = 0.125
TM = ("y", "zl")
SPACE = ("zh", "x", "c")
VMEM_LIMIT = 63 * 1024 * 1024


def params(size=VMEM_LIMIT):
    return pltpu.CompilerParams(vmem_limit_bytes=size)


def cost(micros):
    return pl.CostEstimate(flops=micros * 1000000000, bytes_accessed=0, transcendentals=0)


def whole():
    return pl.BlockSpec()


def in_hbm(value):
    return pltpu.with_memory_space_constraint(value, pltpu.HBM)


def in_vmem(value):
    return pltpu.with_memory_space_constraint(value, pltpu.VMEM)


def resident():
    return pl.BlockSpec(memory_space=pltpu.VMEM)


def smem():
    return pl.BlockSpec(memory_space=pltpu.SMEM)


def hbm():
    return pl.BlockSpec(memory_space=pl.ANY)


def shift(value, axis, step):
    size = lax.axis_size(axis)
    return lax.ppermute(value, axis, [(i, (i + step) % size) for i in range(size)])


def after(value, *others):
    return lax.optimization_barrier((value,) + others)[0]


def swap(pieces):
    return [shift(piece, "c", 1) for piece in pieces]


def spread(value, axis):
    far = shift(value, axis, 2)
    return [shift(value, axis, -1), far, shift(value, axis, 1)]


def gather_frames(keys, values):
    column_k = jnp.concatenate([keys] + spread(keys, "zh"), axis=0)
    column_v = jnp.concatenate([values] + spread(values, "zh"), axis=0)
    rows_k = spread(column_k, "x")
    rows_v = spread(column_v, "x")
    rows_k = lax.optimization_barrier(tuple(rows_k) + (column_v,))[:3]
    pieces_k = [column_k, *rows_k]
    pieces_v = [column_v, *rows_v]
    return pieces_k + swap(pieces_k), pieces_v + swap(pieces_v)


def select_kernel(piece_ref, row_ref, *refs):
    pieces, out_ref, sems = refs[:-2], refs[-2], refs[-1]

    @pl.loop(0, FRAMES * SLOTS)
    def _(slot):
        which = piece_ref[slot]
        row = row_ref[slot]
        for number, piece in enumerate(pieces):

            @pl.when(which == number)
            def _():
                pltpu.make_async_copy(
                    piece.at[pl.ds(row, 1)], out_ref.at[pl.ds(slot, 1)], sems.at[slot]
                ).start()

    @pl.loop(0, FRAMES * SLOTS)
    def _(slot):
        pltpu.make_async_copy(
            pieces[0].at[pl.ds(0, 1)], out_ref.at[pl.ds(slot, 1)], sems.at[slot]
        ).wait()


def select_tiles(piece_ids, piece_rows, pieces, micros=0):
    return pl.pallas_call(
        select_kernel,
        out_shape=jax.ShapeDtypeStruct((FRAMES * SLOTS, TILE, WIDTH), jnp.bfloat16),
        in_specs=[smem(), smem()] + [hbm()] * len(pieces),
        out_specs=whole(),
        scratch_shapes=[pltpu.SemaphoreType.DMA((FRAMES * SLOTS,))],
        compiler_params=params(6 * 1024 * 1024),
        cost_estimate=cost(micros),
        name="select_tiles",
    )(piece_ids, piece_rows, *pieces)


def split_heads(pair):
    rows = lax.broadcasted_iota(jnp.int32, pair.shape, 0)
    zero = jnp.zeros_like(pair)
    return jnp.concatenate(
        [jnp.where(rows < HEAD, pair, zero), jnp.where(rows >= HEAD, pair, zero)], axis=1
    )


def join_heads(both):
    return jnp.concatenate([both[:HEAD, :ROWS], both[HEAD:, ROWS:]], axis=0)


def dot_nn(a, b):
    return jnp.dot(a, b, preferred_element_type=jnp.float32)


def dot_tn(a, b):
    return lax.dot_general(a, b, (((0,), (0,)), ((), ())), preferred_element_type=jnp.float32)


def dot_nt(a, b):
    return lax.dot_general(a, b, (((1,), (1,)), ((), ())), preferred_element_type=jnp.float32)


def weights_kernel(count_ref, query_ref, key_ref, weight_ref, narrow_ref, turned):
    frame = pl.program_id(0)

    @pl.when(frame == 0)
    def _():
        turned[...] = query_ref[...].T

    limit = count_ref[frame] * TILE
    rows = lax.broadcasted_iota(jnp.int32, (ROWS, 2 * ROWS), 0)
    live = rows < limit
    for pair in range(PAIRS):
        lanes = slice(pair * 128, pair * 128 + 128)
        scores = dot_nn(key_ref[0, :, lanes], split_heads(turned[lanes, :])) * SCALE
        scores = jnp.where(live, scores, -jnp.inf)
        raised = jnp.exp(scores - jnp.max(scores, axis=0, keepdims=True))
        weights = raised / jnp.sum(raised, axis=0, keepdims=True)
        weight_ref[0, pair] = weights
        narrow_ref[frame, pair] = weights.astype(jnp.bfloat16)


def attend_weights(counts, queries, keys):
    return pl.pallas_call(
        weights_kernel,
        grid=(FRAMES,),
        out_shape=(
            pltpu.HBM((FRAMES, PAIRS, ROWS, 2 * ROWS), jnp.float32),
            pltpu.VMEM((FRAMES, PAIRS, ROWS, 2 * ROWS), jnp.bfloat16),
        ),
        in_specs=[
            smem(),
            pl.BlockSpec((ROWS, WIDTH), lambda f: (0, 0)),
            pl.BlockSpec((1, ROWS, WIDTH), lambda f: (f, 0, 0)),
        ],
        out_specs=(
            pl.BlockSpec((1, PAIRS, ROWS, 2 * ROWS), lambda f: (f, 0, 0, 0)),
            resident(),
        ),
        scratch_shapes=[pltpu.VMEM((WIDTH, ROWS), jnp.bfloat16)],
        compiler_params=params(8 * 1024 * 1024),
        name="attend_weights",
    )(counts, queries, in_hbm(keys))


def pool_kernel(
    frame_ref,
    weight_ref,
    value_ref,
    wq_ref,
    wk_ref,
    wv_ref,
    go_ref,
    mixed_ref,
    gt_ref,
    dv_ref,
    traj,
    pooled_k,
    pooled_v,
    pooled_q,
    grad_pk,
    grad_pv,
    grad_pq,
    total,
):
    for frame in range(FRAMES):
        for pair in range(PAIRS):
            lanes = slice(pair * 128, pair * 128 + 128)
            both = dot_tn(value_ref[frame, :, lanes], weight_ref[frame, pair])
            traj[lanes, frame * ROWS : (frame + 1) * ROWS] = join_heads(both).astype(jnp.bfloat16)
    own = pl.ds(pl.multiple_of(frame_ref[0] * ROWS, ROWS), ROWS)
    pooled_q[...] = dot_tn(wq_ref[...], traj[:, own])
    pooled_k[...] = dot_tn(wk_ref[...], traj[...])
    pooled_v[...] = dot_tn(wv_ref[...], traj[...])
    upstream_t = go_ref[...].astype(jnp.float32).T
    for head in range(HEADS):
        rows = slice(head * HEAD, (head + 1) * HEAD)
        query = pooled_q[rows, :]
        upstream = upstream_t[rows, :]
        columns = [slice(f * ROWS, (f + 1) * ROWS) for f in range(FRAMES)]
        logits = jnp.concatenate(
            [
                jnp.sum(query * pooled_k[rows, columns[f]], axis=0, keepdims=True)
                for f in range(FRAMES)
            ],
            axis=0,
        )
        raised = jnp.exp(logits * SCALE)
        fw = raised / jnp.sum(raised, axis=0, keepdims=True)
        grad_fw = jnp.concatenate(
            [
                jnp.sum(upstream * pooled_v[rows, columns[f]], axis=0, keepdims=True)
                for f in range(FRAMES)
            ],
            axis=0,
        )
        inner = jnp.sum(fw * grad_fw, axis=0, keepdims=True)
        grad_logit = fw * (grad_fw - inner) * SCALE
        mixed = jnp.zeros((HEAD, ROWS), jnp.float32)
        grad_query = jnp.zeros((HEAD, ROWS), jnp.float32)
        for f in range(FRAMES):
            weight = fw[f : f + 1, :]
            slope = grad_logit[f : f + 1, :]
            mixed = mixed + weight * pooled_v[rows, columns[f]]
            grad_query = grad_query + slope * pooled_k[rows, columns[f]]
            grad_pk[rows, columns[f]] = (slope * query).astype(jnp.bfloat16)
            grad_pv[rows, columns[f]] = (weight * upstream).astype(jnp.bfloat16)
        pooled_q[rows, :] = mixed
        grad_pq[rows, :] = grad_query.astype(jnp.bfloat16)
    mixed_ref[...] = pooled_q[...].T.astype(jnp.bfloat16)
    total[...] = dot_nn(wk_ref[...], grad_pk[...]) + dot_nn(wv_ref[...], grad_pv[...])
    total[:, own] += dot_nn(wq_ref[...], grad_pq[...])
    for frame in range(FRAMES):
        gt_ref[frame] = total[:, frame * ROWS : (frame + 1) * ROWS].astype(jnp.bfloat16)
        for pair in range(PAIRS):
            lanes = slice(pair * 128, pair * 128 + 128)
            dv_ref[frame, :, lanes] = dot_nt(
                weight_ref[frame, pair], split_heads(gt_ref[frame, lanes, :])
            ).astype(jnp.bfloat16)


def pool_frames(frame_now, weights, values, w_query, w_key, w_value, upstream):
    wide = (WIDTH, FRAMES * ROWS)
    return pl.pallas_call(
        pool_kernel,
        out_shape=(
            pltpu.HBM((ROWS, WIDTH), jnp.bfloat16),
            pltpu.HBM((FRAMES, WIDTH, ROWS), jnp.bfloat16),
            pltpu.HBM((FRAMES, ROWS, WIDTH), jnp.bfloat16),
        ),
        in_specs=[smem(), resident()] + [whole()] * 5,
        out_specs=(whole(), whole(), whole()),
        scratch_shapes=[
            pltpu.VMEM(wide, jnp.bfloat16),
            pltpu.VMEM(wide, jnp.float32),
            pltpu.VMEM(wide, jnp.float32),
            pltpu.VMEM((WIDTH, ROWS), jnp.float32),
            pltpu.VMEM(wide, jnp.bfloat16),
            pltpu.VMEM(wide, jnp.bfloat16),
            pltpu.VMEM((WIDTH, ROWS), jnp.bfloat16),
            pltpu.VMEM(wide, jnp.float32),
        ],
        compiler_params=params(18 * 1024 * 1024),
        name="pool_frames",
    )(
        frame_now.reshape(1),
        in_vmem(weights),
        in_hbm(values),
        in_hbm(w_query),
        in_hbm(w_key),
        in_hbm(w_value),
        in_hbm(upstream),
    )


def back_kernel(query_ref, key_ref, value_ref, weight_ref, gt_ref, gq_ref, dk_ref, turned, total):
    frame = pl.program_id(0)

    @pl.when(frame == 0)
    def _():
        total[...] = jnp.zeros_like(total)
        turned[...] = query_ref[...].T

    for pair in range(PAIRS):
        lanes = slice(pair * 128, pair * 128 + 128)
        weight = weight_ref[0, pair]
        grad_w = dot_nn(value_ref[0, :, lanes], split_heads(gt_ref[0, lanes, :]))
        inner = jnp.sum(weight * grad_w, axis=0, keepdims=True)
        grad_s = (weight * (grad_w - inner) * SCALE).astype(jnp.bfloat16)
        dk_ref[0, :, lanes] = dot_nt(grad_s, split_heads(turned[lanes, :])).astype(jnp.bfloat16)
        total[lanes, :] += join_heads(dot_tn(key_ref[0, :, lanes], grad_s))

    @pl.when(frame == FRAMES - 1)
    def _():
        gq_ref[...] = total[...].T.astype(jnp.bfloat16)


def attend_back(queries, keys, values, weights, grad_traj):
    by_frame = pl.BlockSpec((1, ROWS, WIDTH), lambda f: (f, 0, 0))
    fixed = pl.BlockSpec((ROWS, WIDTH), lambda f: (0, 0))
    return pl.pallas_call(
        back_kernel,
        grid=(FRAMES,),
        out_shape=(
            pltpu.HBM((ROWS, WIDTH), jnp.bfloat16),
            pltpu.HBM((FRAMES, ROWS, WIDTH), jnp.bfloat16),
        ),
        in_specs=[
            fixed,
            by_frame,
            by_frame,
            pl.BlockSpec((1, PAIRS, ROWS, 2 * ROWS), lambda f: (f, 0, 0, 0)),
            pl.BlockSpec((1, WIDTH, ROWS), lambda f: (f, 0, 0)),
        ],
        out_specs=(fixed, by_frame),
        scratch_shapes=[
            pltpu.VMEM((WIDTH, ROWS), jnp.bfloat16),
            pltpu.VMEM((WIDTH, ROWS), jnp.float32),
        ],
        compiler_params=params(10 * 1024 * 1024),
        name="attend_back",
    )(queries, in_hbm(keys), in_hbm(values), in_hbm(weights), in_hbm(grad_traj))


def merge_kernel(place_ref, mine_ref, theirs_ref, *refs):
    outs, acc = refs[:5], refs[5]
    acc[...] = jnp.zeros_like(acc)
    for source, ref in enumerate((mine_ref, theirs_ref)):

        @pl.loop(0, FRAMES * SLOTS)
        def _(slot):
            place = place_ref[source * FRAMES * SLOTS + slot]

            @pl.when(place >= 0)
            def _():
                acc[place] += ref[slot].astype(jnp.float32)

    at = 0
    for out in outs:
        size = out.shape[0]
        out[...] = acc[at : at + size].astype(jnp.bfloat16)
        at += size


def merge_slots(places, mine, theirs):
    sizes = (8, 8, 4, 4, 8)
    return pl.pallas_call(
        merge_kernel,
        out_shape=tuple(jax.ShapeDtypeStruct((n, TILE, WIDTH), jnp.bfloat16) for n in sizes),
        in_specs=[smem(), whole(), whole()],
        out_specs=(whole(),) * 5,
        scratch_shapes=[pltpu.VMEM((32, TILE, WIDTH), jnp.float32)],
        compiler_params=params(),
        name="merge_slots",
    )(places, mine, theirs)


def add_wide(*terms):
    total = terms[0].astype(jnp.float32)
    for term in terms[1:]:
        total = total + term.astype(jnp.float32)
    return total.astype(jnp.bfloat16)


def scatter_rows(merged):
    to_right, to_left, keep_right, keep_left, own = merged
    from_left = shift(to_right, "x", 1)
    from_right = shift(to_left, "x", -1)
    return keep_right, keep_left, own, from_left, from_right


def scatter_across(state):
    keep_right, keep_left, own, from_left, from_right = state
    low = shift(add_wide(keep_right, from_left[0:4]), "x", 1)
    high = shift(add_wide(keep_left, from_right[0:4]), "x", -1)
    return own, from_left, from_right, low, high


def scatter_column(state):
    own, from_left, from_right, low, high = state
    here = add_wide(own[0:2], from_right[4:6], low[0:2])
    up = add_wide(own[2:4], from_right[6:8], low[2:4])
    far = add_wide(own[4:6], from_left[4:6], high[0:2])
    down = add_wide(own[6:8], from_left[6:8], high[2:4])
    return add_wide(here, shift(up, "zh", 1), shift(far, "zh", 2), shift(down, "zh", -1))


def per_device(queries, keys, values, w_query, w_key, w_value, grad_out, tile_list, tile_count):
    frame_now = lax.axis_index("y") * 2 + lax.axis_index("zl")
    at_z, at_x, at_c = (lax.axis_index(a) for a in SPACE)
    my_space = (at_z * 4 + at_x) * 2 + at_c
    pair_space = (at_z * 4 + at_x) * 2

    wanted = lax.dynamic_slice(
        tile_list, (0, pair_space, frame_now, 0), (FRAMES, 2, 1, SLOTS)
    ).reshape(FRAMES, 2, SLOTS)
    wanted = wanted.transpose(1, 0, 2).reshape(2, FRAMES * SLOTS)
    mine_wanted = lax.dynamic_index_in_dim(wanted, at_c, 0, keepdims=False)
    their_wanted = lax.dynamic_index_in_dim(wanted, 1 - at_c, 0, keepdims=False)

    def locate(tiles):
        owner = tiles // 2
        z_rel = (owner // 8 - at_z) % 4
        x_rel = (owner // 2 % 4 - at_x) % 4
        other = (owner % 2 != at_c).astype(jnp.int32)
        return z_rel * 2 + tiles % 2, x_rel, other

    inside, x_rel, other = locate(mine_wanted)
    piece_ids = x_rel + 4 * other

    def placing(tiles):
        inside, x_rel, other = locate(tiles)
        high = inside >= 4
        low_part = inside % 4
        place = jnp.where(
            x_rel == 0,
            24 + inside,
            jnp.where(
                x_rel == 1,
                jnp.where(high, 4 + low_part, 16 + low_part),
                jnp.where(
                    x_rel == 2,
                    jnp.where(high, 8 + low_part, low_part),
                    jnp.where(high, 20 + low_part, 12 + low_part),
                ),
            ),
        )
        return jnp.where(other == 1, -1, place)

    places = jnp.concatenate([placing(mine_wanted), placing(their_wanted)])

    def exchange(chosen):
        return lax.all_to_all(
            chosen.reshape(FRAMES, SLOTS * TILE, WIDTH), TM, split_axis=0, concat_axis=0, tiled=True
        )

    counts = lax.dynamic_slice(tile_count, (frame_now, my_space, 0), (1, 1, FRAMES)).reshape(FRAMES)
    query_rows = queries.reshape(ROWS, WIDTH)
    upstream_rows = grad_out.reshape(ROWS, WIDTH)
    own_shape = (2, TILE, WIDTH)
    key_pieces, value_pieces = gather_frames(keys.reshape(own_shape), values.reshape(own_shape))
    key_slots = exchange(select_tiles(piece_ids, inside, key_pieces))
    value_slots = exchange(select_tiles(piece_ids, inside, value_pieces, 13))
    weights, narrow = attend_weights(counts, query_rows, key_slots)
    mixed, grad_traj, slot_dv = pool_frames(
        frame_now, narrow, value_slots, w_query, w_key, w_value, upstream_rows
    )
    grad_queries, slot_dk = attend_back(query_rows, key_slots, value_slots, weights, grad_traj)
    owned_v = exchange(slot_dv).reshape(FRAMES * SLOTS, TILE, WIDTH)
    owned_v = after(owned_v, slot_dk)
    merged_v = merge_slots(places, owned_v, shift(owned_v, "c", 1))
    owned_k = exchange(slot_dk).reshape(FRAMES * SLOTS, TILE, WIDTH)
    owned_k = after(owned_k, *merged_v)
    state_v = scatter_rows(merged_v)
    merged_k = merge_slots(places, owned_k, shift(owned_k, "c", 1))
    state_k = scatter_rows(merged_k)
    state_v = lax.optimization_barrier(state_v + (merged_k[0],))[:5]
    state_v = scatter_across(state_v)
    state_k = scatter_across(state_k)
    sum_values = scatter_column(state_v)
    sum_keys = scatter_column(state_k)
    shape = (1, ROWS, WIDTH)
    return (
        mixed.reshape(shape),
        grad_queries.reshape(shape),
        sum_keys.reshape(shape),
        sum_values.reshape(shape),
    )


def solution(mesh):
    fine = Mesh(mesh.devices.reshape(4, 2, 4, 4, 2), TM + SPACE)
    rows = P(TM, SPACE, None)
    return jax.shard_map(
        per_device,
        mesh=fine,
        in_specs=(rows, rows, rows, P(), P(), P(), rows, P(), P()),
        out_specs=(rows, rows, rows, rows),
        check_vma=False,
    )
```

```python
import functools

import jax
import jax.numpy as jnp
from jax import lax
from jax.experimental import pallas as pl
from jax.experimental.pallas import tpu as pltpu
from jax.sharding import Mesh
from jax.sharding import PartitionSpec as P

HEAD = 64
HEADS = 8
TILE = 64
FRAMES = 8
SLOTS = 2
WIDTH = 512
PAIRS = 4
ROWS = 128
SCALE = 0.125
TM = ("y", "zl")
SPACE = ("zh", "x", "c")
VMEM_LIMIT = 63 * 1024 * 1024


def params(size=VMEM_LIMIT):
    return pltpu.CompilerParams(vmem_limit_bytes=size)


def cost(micros):
    return pl.CostEstimate(flops=micros * 1000000000, bytes_accessed=0, transcendentals=0)


def whole():
    return pl.BlockSpec()


def in_hbm(value):
    return pltpu.with_memory_space_constraint(value, pltpu.HBM)


def in_vmem(value):
    return pltpu.with_memory_space_constraint(value, pltpu.VMEM)


def resident():
    return pl.BlockSpec(memory_space=pltpu.VMEM)


def smem():
    return pl.BlockSpec(memory_space=pltpu.SMEM)


def hbm():
    return pl.BlockSpec(memory_space=pl.ANY)


def shift(value, axis, step):
    size = lax.axis_size(axis)
    return lax.ppermute(value, axis, [(i, (i + step) % size) for i in range(size)])


def after(value, *others):
    return lax.optimization_barrier((value,) + others)[0]


def swap(pieces):
    return [shift(piece, "c", 1) for piece in pieces]


def spread(value, axis):
    far = shift(value, axis, 2)
    return [shift(value, axis, -1), far, shift(value, axis, 1)]


def gather_frames(keys, values):
    column_k = jnp.concatenate([keys] + spread(keys, "zh"), axis=0)
    column_v = jnp.concatenate([values] + spread(values, "zh"), axis=0)
    rows_k = spread(column_k, "x")
    rows_v = spread(column_v, "x")
    rows_k = lax.optimization_barrier(tuple(rows_k) + (column_v,))[:3]
    pieces_k = [column_k, *rows_k]
    pieces_v = [column_v, *rows_v]
    return pieces_k + swap(pieces_k), pieces_v + swap(pieces_v)


def select_kernel(piece_ref, row_ref, *refs):
    pieces, out_ref, sems = refs[:-2], refs[-2], refs[-1]

    @pl.loop(0, FRAMES * SLOTS)
    def _(slot):
        which = piece_ref[slot]
        row = row_ref[slot]
        for number, piece in enumerate(pieces):

            @pl.when(which == number)
            def _():
                pltpu.make_async_copy(
                    piece.at[pl.ds(row, 1)], out_ref.at[pl.ds(slot, 1)], sems.at[slot]
                ).start()

    @pl.loop(0, FRAMES * SLOTS)
    def _(slot):
        pltpu.make_async_copy(
            pieces[0].at[pl.ds(0, 1)], out_ref.at[pl.ds(slot, 1)], sems.at[slot]
        ).wait()


def select_tiles(piece_ids, piece_rows, pieces, micros=0):
    return pl.pallas_call(
        select_kernel,
        out_shape=jax.ShapeDtypeStruct((FRAMES * SLOTS, TILE, WIDTH), jnp.bfloat16),
        in_specs=[smem(), smem()] + [hbm()] * len(pieces),
        out_specs=whole(),
        scratch_shapes=[pltpu.SemaphoreType.DMA((FRAMES * SLOTS,))],
        compiler_params=params(6 * 1024 * 1024),
        cost_estimate=cost(micros),
        name="select_tiles",
    )(piece_ids, piece_rows, *pieces)


def split_heads(pair):
    rows = lax.broadcasted_iota(jnp.int32, pair.shape, 0)
    zero = jnp.zeros_like(pair)
    return jnp.concatenate(
        [jnp.where(rows < HEAD, pair, zero), jnp.where(rows >= HEAD, pair, zero)], axis=1
    )


def join_heads(both):
    return jnp.concatenate([both[:HEAD, :ROWS], both[HEAD:, ROWS:]], axis=0)


def dot_nn(a, b):
    return jnp.dot(a, b, preferred_element_type=jnp.float32)


def dot_tn(a, b):
    return lax.dot_general(a, b, (((0,), (0,)), ((), ())), preferred_element_type=jnp.float32)


def dot_nt(a, b):
    return lax.dot_general(a, b, (((1,), (1,)), ((), ())), preferred_element_type=jnp.float32)


def weights_kernel(count_ref, query_ref, key_ref, weight_ref, narrow_ref, turned):
    frame = pl.program_id(0)

    @pl.when(frame == 0)
    def _():
        turned[...] = query_ref[...].T

    limit = count_ref[frame] * TILE
    rows = lax.broadcasted_iota(jnp.int32, (ROWS, 2 * ROWS), 0)
    live = rows < limit
    for pair in range(PAIRS):
        lanes = slice(pair * 128, pair * 128 + 128)
        scores = dot_nn(key_ref[0, :, lanes], split_heads(turned[lanes, :])) * SCALE
        scores = jnp.where(live, scores, -jnp.inf)
        raised = jnp.exp(scores - jnp.max(scores, axis=0, keepdims=True))
        weights = raised / jnp.sum(raised, axis=0, keepdims=True)
        weight_ref[0, pair] = weights
        narrow_ref[frame, pair] = weights.astype(jnp.bfloat16)


def attend_weights(counts, queries, keys):
    return pl.pallas_call(
        weights_kernel,
        grid=(FRAMES,),
        out_shape=(
            pltpu.HBM((FRAMES, PAIRS, ROWS, 2 * ROWS), jnp.float32),
            pltpu.VMEM((FRAMES, PAIRS, ROWS, 2 * ROWS), jnp.bfloat16),
        ),
        in_specs=[
            smem(),
            pl.BlockSpec((ROWS, WIDTH), lambda f: (0, 0)),
            pl.BlockSpec((1, ROWS, WIDTH), lambda f: (f, 0, 0)),
        ],
        out_specs=(
            pl.BlockSpec((1, PAIRS, ROWS, 2 * ROWS), lambda f: (f, 0, 0, 0)),
            resident(),
        ),
        scratch_shapes=[pltpu.VMEM((WIDTH, ROWS), jnp.bfloat16)],
        compiler_params=params(8 * 1024 * 1024),
        name="attend_weights",
    )(counts, queries, in_hbm(keys))


def pool_kernel(
    frame_ref,
    weight_ref,
    value_ref,
    wq_ref,
    wk_ref,
    wv_ref,
    go_ref,
    mixed_ref,
    gt_ref,
    dv_ref,
    traj,
    pooled_k,
    pooled_v,
    pooled_q,
    grad_pk,
    grad_pv,
    grad_pq,
    total,
):
    for frame in range(FRAMES):
        for pair in range(PAIRS):
            lanes = slice(pair * 128, pair * 128 + 128)
            both = dot_tn(value_ref[frame, :, lanes], weight_ref[frame, pair])
            traj[lanes, frame * ROWS : (frame + 1) * ROWS] = join_heads(both).astype(jnp.bfloat16)
    own = pl.ds(pl.multiple_of(frame_ref[0] * ROWS, ROWS), ROWS)
    pooled_q[...] = dot_tn(wq_ref[...], traj[:, own])
    pooled_k[...] = dot_tn(wk_ref[...], traj[...])
    pooled_v[...] = dot_tn(wv_ref[...], traj[...])
    upstream_t = go_ref[...].astype(jnp.float32).T
    for head in range(HEADS):
        rows = slice(head * HEAD, (head + 1) * HEAD)
        query = pooled_q[rows, :]
        upstream = upstream_t[rows, :]
        columns = [slice(f * ROWS, (f + 1) * ROWS) for f in range(FRAMES)]
        logits = jnp.concatenate(
            [
                jnp.sum(query * pooled_k[rows, columns[f]], axis=0, keepdims=True)
                for f in range(FRAMES)
            ],
            axis=0,
        )
        raised = jnp.exp(logits * SCALE)
        fw = raised / jnp.sum(raised, axis=0, keepdims=True)
        grad_fw = jnp.concatenate(
            [
                jnp.sum(upstream * pooled_v[rows, columns[f]], axis=0, keepdims=True)
                for f in range(FRAMES)
            ],
            axis=0,
        )
        inner = jnp.sum(fw * grad_fw, axis=0, keepdims=True)
        grad_logit = fw * (grad_fw - inner) * SCALE
        mixed = jnp.zeros((HEAD, ROWS), jnp.float32)
        grad_query = jnp.zeros((HEAD, ROWS), jnp.float32)
        for f in range(FRAMES):
            weight = fw[f : f + 1, :]
            slope = grad_logit[f : f + 1, :]
            mixed = mixed + weight * pooled_v[rows, columns[f]]
            grad_query = grad_query + slope * pooled_k[rows, columns[f]]
            grad_pk[rows, columns[f]] = (slope * query).astype(jnp.bfloat16)
            grad_pv[rows, columns[f]] = (weight * upstream).astype(jnp.bfloat16)
        pooled_q[rows, :] = mixed
        grad_pq[rows, :] = grad_query.astype(jnp.bfloat16)
    mixed_ref[...] = pooled_q[...].T.astype(jnp.bfloat16)
    total[...] = dot_nn(wk_ref[...], grad_pk[...]) + dot_nn(wv_ref[...], grad_pv[...])
    total[:, own] += dot_nn(wq_ref[...], grad_pq[...])
    for frame in range(FRAMES):
        gt_ref[frame] = total[:, frame * ROWS : (frame + 1) * ROWS].astype(jnp.bfloat16)
        for pair in range(PAIRS):
            lanes = slice(pair * 128, pair * 128 + 128)
            dv_ref[frame, :, lanes] = dot_nt(
                weight_ref[frame, pair], split_heads(gt_ref[frame, lanes, :])
            ).astype(jnp.bfloat16)


def pool_frames(frame_now, weights, values, w_query, w_key, w_value, upstream):
    wide = (WIDTH, FRAMES * ROWS)
    return pl.pallas_call(
        pool_kernel,
        out_shape=(
            pltpu.HBM((ROWS, WIDTH), jnp.bfloat16),
            pltpu.HBM((FRAMES, WIDTH, ROWS), jnp.bfloat16),
            pltpu.HBM((FRAMES, ROWS, WIDTH), jnp.bfloat16),
        ),
        in_specs=[smem(), resident()] + [whole()] * 5,
        out_specs=(whole(), whole(), whole()),
        scratch_shapes=[
            pltpu.VMEM(wide, jnp.bfloat16),
            pltpu.VMEM(wide, jnp.float32),
            pltpu.VMEM(wide, jnp.float32),
            pltpu.VMEM((WIDTH, ROWS), jnp.float32),
            pltpu.VMEM(wide, jnp.bfloat16),
            pltpu.VMEM(wide, jnp.bfloat16),
            pltpu.VMEM((WIDTH, ROWS), jnp.bfloat16),
            pltpu.VMEM(wide, jnp.float32),
        ],
        compiler_params=params(18 * 1024 * 1024),
        name="pool_frames",
    )(
        frame_now.reshape(1),
        in_vmem(weights),
        in_hbm(values),
        in_hbm(w_query),
        in_hbm(w_key),
        in_hbm(w_value),
        in_hbm(upstream),
    )


def back_kernel(query_ref, key_ref, value_ref, weight_ref, gt_ref, gq_ref, dk_ref, turned, total):
    frame = pl.program_id(0)

    @pl.when(frame == 0)
    def _():
        total[...] = jnp.zeros_like(total)
        turned[...] = query_ref[...].T

    for pair in range(PAIRS):
        lanes = slice(pair * 128, pair * 128 + 128)
        weight = weight_ref[0, pair]
        grad_w = dot_nn(value_ref[0, :, lanes], split_heads(gt_ref[0, lanes, :]))
        inner = jnp.sum(weight * grad_w, axis=0, keepdims=True)
        grad_s = (weight * (grad_w - inner) * SCALE).astype(jnp.bfloat16)
        dk_ref[0, :, lanes] = dot_nt(grad_s, split_heads(turned[lanes, :])).astype(jnp.bfloat16)
        total[lanes, :] += join_heads(dot_tn(key_ref[0, :, lanes], grad_s))

    @pl.when(frame == FRAMES - 1)
    def _():
        gq_ref[...] = total[...].T.astype(jnp.bfloat16)


def attend_back(queries, keys, values, weights, grad_traj):
    by_frame = pl.BlockSpec((1, ROWS, WIDTH), lambda f: (f, 0, 0))
    fixed = pl.BlockSpec((ROWS, WIDTH), lambda f: (0, 0))
    return pl.pallas_call(
        back_kernel,
        grid=(FRAMES,),
        out_shape=(
            pltpu.HBM((ROWS, WIDTH), jnp.bfloat16),
            pltpu.HBM((FRAMES, ROWS, WIDTH), jnp.bfloat16),
        ),
        in_specs=[
            fixed,
            by_frame,
            by_frame,
            pl.BlockSpec((1, PAIRS, ROWS, 2 * ROWS), lambda f: (f, 0, 0, 0)),
            pl.BlockSpec((1, WIDTH, ROWS), lambda f: (f, 0, 0)),
        ],
        out_specs=(fixed, by_frame),
        scratch_shapes=[
            pltpu.VMEM((WIDTH, ROWS), jnp.bfloat16),
            pltpu.VMEM((WIDTH, ROWS), jnp.float32),
        ],
        compiler_params=params(10 * 1024 * 1024),
        name="attend_back",
    )(queries, in_hbm(keys), in_hbm(values), in_hbm(weights), in_hbm(grad_traj))


def merge_kernel(place_ref, mine_ref, theirs_ref, *refs):
    outs, acc = refs[:5], refs[5]
    acc[...] = jnp.zeros_like(acc)
    for source, ref in enumerate((mine_ref, theirs_ref)):

        @pl.loop(0, FRAMES * SLOTS)
        def _(slot):
            place = place_ref[source * FRAMES * SLOTS + slot]

            @pl.when(place >= 0)
            def _():
                acc[place] += ref[slot].astype(jnp.float32)

    at = 0
    for out in outs:
        size = out.shape[0]
        out[...] = acc[at : at + size].astype(jnp.bfloat16)
        at += size


def merge_slots(places, mine, theirs):
    sizes = (8, 8, 4, 4, 8)
    half = WIDTH // 2
    slots = pl.BlockSpec((FRAMES * SLOTS, TILE, half), lambda i: (0, 0, i))
    return pl.pallas_call(
        merge_kernel,
        grid=(2,),
        out_shape=tuple(jax.ShapeDtypeStruct((n, TILE, WIDTH), jnp.bfloat16) for n in sizes),
        in_specs=[smem(), slots, slots],
        out_specs=tuple(pl.BlockSpec((n, TILE, half), lambda i: (0, 0, i)) for n in sizes),
        scratch_shapes=[pltpu.VMEM((32, TILE, half), jnp.float32)],
        compiler_params=params(),
        name="merge_slots",
    )(places, mine, theirs)


def add_wide(*terms):
    total = terms[0].astype(jnp.float32)
    for term in terms[1:]:
        total = total + term.astype(jnp.float32)
    return total.astype(jnp.bfloat16)


def scatter_rows(merged):
    to_right, to_left, keep_right, keep_left, own = merged
    from_left = shift(to_right, "x", 1)
    from_right = shift(to_left, "x", -1)
    return keep_right, keep_left, own, from_left, from_right


def scatter_across(state):
    keep_right, keep_left, own, from_left, from_right = state
    low = shift(add_wide(keep_right, from_left[0:4]), "x", 1)
    high = shift(add_wide(keep_left, from_right[0:4]), "x", -1)
    return own, from_left, from_right, low, high


def scatter_column(state):
    own, from_left, from_right, low, high = state
    here = add_wide(own[0:2], from_right[4:6], low[0:2])
    up = add_wide(own[2:4], from_right[6:8], low[2:4])
    far = add_wide(own[4:6], from_left[4:6], high[0:2])
    down = add_wide(own[6:8], from_left[6:8], high[2:4])
    return add_wide(here, shift(up, "zh", 1), shift(far, "zh", 2), shift(down, "zh", -1))


def per_device(queries, keys, values, w_query, w_key, w_value, grad_out, tile_list, tile_count):
    frame_now = lax.axis_index("y") * 2 + lax.axis_index("zl")
    at_z, at_x, at_c = (lax.axis_index(a) for a in SPACE)
    my_space = (at_z * 4 + at_x) * 2 + at_c
    pair_space = (at_z * 4 + at_x) * 2

    wanted = lax.dynamic_slice(
        tile_list, (0, pair_space, frame_now, 0), (FRAMES, 2, 1, SLOTS)
    ).reshape(FRAMES, 2, SLOTS)
    wanted = wanted.transpose(1, 0, 2).reshape(2, FRAMES * SLOTS)
    mine_wanted = lax.dynamic_index_in_dim(wanted, at_c, 0, keepdims=False)
    their_wanted = lax.dynamic_index_in_dim(wanted, 1 - at_c, 0, keepdims=False)

    def locate(tiles):
        owner = tiles // 2
        z_rel = (owner // 8 - at_z) % 4
        x_rel = (owner // 2 % 4 - at_x) % 4
        other = (owner % 2 != at_c).astype(jnp.int32)
        return z_rel * 2 + tiles % 2, x_rel, other

    inside, x_rel, other = locate(mine_wanted)
    piece_ids = x_rel + 4 * other

    def placing(tiles):
        inside, x_rel, other = locate(tiles)
        high = inside >= 4
        low_part = inside % 4
        place = jnp.where(
            x_rel == 0,
            24 + inside,
            jnp.where(
                x_rel == 1,
                jnp.where(high, 4 + low_part, 16 + low_part),
                jnp.where(
                    x_rel == 2,
                    jnp.where(high, 8 + low_part, low_part),
                    jnp.where(high, 20 + low_part, 12 + low_part),
                ),
            ),
        )
        return jnp.where(other == 1, -1, place)

    places = jnp.concatenate([placing(mine_wanted), placing(their_wanted)])

    def exchange(chosen):
        return lax.all_to_all(
            chosen.reshape(FRAMES, SLOTS * TILE, WIDTH), TM, split_axis=0, concat_axis=0, tiled=True
        )

    counts = lax.dynamic_slice(tile_count, (frame_now, my_space, 0), (1, 1, FRAMES)).reshape(FRAMES)
    query_rows = queries.reshape(ROWS, WIDTH)
    upstream_rows = grad_out.reshape(ROWS, WIDTH)
    own_shape = (2, TILE, WIDTH)
    key_pieces, value_pieces = gather_frames(keys.reshape(own_shape), values.reshape(own_shape))
    key_slots = exchange(select_tiles(piece_ids, inside, key_pieces))
    value_slots = exchange(select_tiles(piece_ids, inside, value_pieces, 13))
    weights, narrow = attend_weights(counts, query_rows, key_slots)
    mixed, grad_traj, slot_dv = pool_frames(
        frame_now, narrow, value_slots, w_query, w_key, w_value, upstream_rows
    )
    grad_queries, slot_dk = attend_back(query_rows, key_slots, value_slots, weights, grad_traj)
    owned_v = exchange(slot_dv).reshape(FRAMES * SLOTS, TILE, WIDTH)
    owned_v = after(owned_v, slot_dk)
    merged_v = merge_slots(places, owned_v, shift(owned_v, "c", 1))
    owned_k = exchange(slot_dk).reshape(FRAMES * SLOTS, TILE, WIDTH)
    owned_k = after(owned_k, *merged_v)
    state_v = scatter_rows(merged_v)
    merged_k = merge_slots(places, owned_k, shift(owned_k, "c", 1))
    state_k = scatter_rows(merged_k)
    state_v = lax.optimization_barrier(state_v + (merged_k[0],))[:5]
    state_v = scatter_across(state_v)
    state_k = scatter_across(state_k)
    sum_values = scatter_column(state_v)
    sum_keys = scatter_column(state_k)
    shape = (1, ROWS, WIDTH)
    return (
        mixed.reshape(shape),
        grad_queries.reshape(shape),
        sum_keys.reshape(shape),
        sum_values.reshape(shape),
    )


def solution(mesh):
    fine = Mesh(mesh.devices.reshape(4, 2, 4, 4, 2), TM + SPACE)
    rows = P(TM, SPACE, None)
    return jax.shard_map(
        per_device,
        mesh=fine,
        in_specs=(rows, rows, rows, P(), P(), P(), rows, P(), P()),
        out_specs=(rows, rows, rows, rows),
        check_vma=False,
    )
```
